512 devices in a mesh: dp: 4 (over y), seq: 16 (over z), expert: 8 (over x, core).
Axes of the slice: x: 4, y: 4, z: 16, core: 2. Of those that a mesh axis runs over, the one named last changes fastest.
Arguments:
- moe_cotangent: bfloat16 [4096, 4096], P(('dp', 'seq', 'expert')), may hold values from -6 to 6
- route_ids: int32 [4096, 2], P(('dp', 'seq', 'expert')), may hold values from 0 to 7, all different within a row; in each aligned block of 8 rows (0 to 7, 8 to 15, ...) at most 2 rows name the same one
- route_weights: bfloat16 [4096, 2], P(('dp', 'seq', 'expert')), may hold values from 0.099609375 to 0.8984375
- saved_pre: bfloat16 [8, 1024, 12288], P('expert', None, ('dp', 'seq')), may hold values from -24 to 24
- w_down: bfloat16 [8, 12288, 4096], P('expert', ('dp', 'seq')), may hold values from -0.0546875 to 0.0546875
- inputs: bfloat16 [4096, 8192], P('seq', ('dp', 'expert')), may hold values from -6 to 6
- deltas: bfloat16 [4096, 8192], P('seq', ('dp', 'expert')), may hold values from 0.25 to 2
- mamba_cotangent: bfloat16 [4096, 8192], P('seq', ('dp', 'expert')), may hold values from -6 to 6
- b_proj: float32 [4096, 16], P('seq'), may hold values from -6 to 6
- c_proj: float32 [4096, 16], P('seq'), may hold values from -6 to 6
- decay_rates: float32 [16, 8192], P(None, ('dp', 'expert')), may hold values from 2.4414063e-05 to 0.2
- skip_gain: float32 [8192], P(('dp', 'expert')), may hold values from 0.5 to 1.5
- documents: int32 [4096], P('seq'), may hold values from 0 to 3, as said below
Outputs:
- w_down_grad: bfloat16 [8, 12288, 4096], P('expert', ('dp', 'seq'))
- route_grad: float32 [4096, 2], P(('dp', 'seq', 'expert'))
- pre_grad: bfloat16 [8, 1024, 12288], P('expert', None, ('dp', 'seq'))
- input_grad: bfloat16 [4096, 8192], P('seq', ('dp', 'expert'))
- delta_grad: bfloat16 [4096, 8192], P('seq', ('dp', 'expert'))
- b_grad: float32 [4096, 16], P('seq')
- c_grad: float32 [4096, 16], P('seq')
- rate_grad: float32 [16, 8192], P(None, ('dp', 'expert'))
- skip_grad: float32 [8192], P(('dp', 'expert'))
The draws below stay inside these ranges and needn't reach their ends.
Inputs may be any that keep to these rules, and one draw needn't show every extreme that they name: `route_ids`: in every aligned block of 8 rows (the rows of one device) no expert is named by more than 2 rows, a bound that some block reaches. `documents`: the numbers never fall, start at 0 and step by one; every document covers one token or more.
All inputs are finite; a program needn't handle non-finite values.
Results may differ from the reference program's by a relative error of at most 0.00225.
The reference program's roundings to bfloat16 on the way (of `received`, `hidden` and `scaled`) count: a program that leaves them out, or rounds other values in their place, can miss the bound.
Values may be sent and summed in bfloat16 or wider, within the bound.
A program may use at most 64 MiB of HBM per device.

```python
import math
import jax
import jax.numpy as jnp
import numpy as np
from jax import lax

D = 4096
FF = 12288
NST = 16
MCH = 8192
TOP = 2
MTOK = 8
EXPERTS = 8
CAP = 2
ROWS = 1024
TOK = 256
LENGTH = 4096
N_DP = 4
N_SEQ = 16
N_EXPERT = 8


def draw_documents(key, part):
    key = jax.random.fold_in(key, 7)
    first_key, second_key, third_key = jax.random.split(key, 3)
    middle = LENGTH // TOK // 2
    first = jax.random.randint(first_key, (), 1, TOK // 2 + 1)
    second = jax.random.randint(second_key, (), middle * TOK + TOK // 2, middle * TOK + TOK)
    third = jax.random.randint(third_key, (), second + 1, LENGTH)
    position = jnp.arange(LENGTH, dtype=jnp.int32)
    numbers = (position >= first).astype(jnp.int32) + (position >= second).astype(jnp.int32) + (position >= third).astype(jnp.int32)
    return numbers.astype(jnp.int32)


def strengthened(entries, own_key, source, target, parts, factor):
    def block_of(dim):
        return (jnp.arange(entries.shape[dim]) // (entries.shape[dim] // parts)).reshape((-1,) + (1,) * (entries.ndim - 1 - dim))

    near = jax.random.permutation(own_key, parts)[block_of(target)]
    other_side = (block_of(target) + parts // 2) % parts
    return jnp.where((block_of(source) == near) | (block_of(source) == other_side), factor * entries, entries)


def block_levels(own_key, shape, shards, low, top_value):
    level, own = 1.0, jax.random.fold_in(own_key, 6)
    for dim, blocks in shards:
        steps = jnp.exp(jax.random.uniform(jax.random.fold_in(own, dim), (blocks,), jnp.float32, low / len(shards), top_value / len(shards)))
        level = level * jnp.repeat(steps, shape[dim] // blocks).reshape([-1 if axis == dim else 1 for axis in range(len(shape))])
    return level


def deal_out(rng, own, number, rows, amount, top, most, slope):
    order = jax.random.permutation(rng, amount)
    crowded, usual = load_shares(amount, rows * top, most, slope, True), load_shares(amount, rows * top, most, slope, False)
    places = jnp.arange(amount)

    def named(lengths, turn):
        used = int((lengths > 0).sum())
        fixed = max(1, used // 4)
        passed = fixed + (places - fixed + turn * (used - fixed)) % max(1, amount - fixed)
        return jnp.zeros((amount,), jnp.int32).at[order[jnp.where(places < fixed, places, passed)]].set(jnp.asarray(lengths, jnp.int32))

    lengths = jnp.where(number % 4 == 0, named(crowded, number // 4), named(usual, number - number // 4 - 1))
    mixed = jax.random.permutation(jax.random.fold_in(own, 3), amount)
    source_of, receiver = mixed[0:amount // 2 * 2:2], mixed[1:amount // 2 * 2:2]
    slack = jnp.minimum(lengths[source_of] - 1, most - lengths[receiver]) // 2
    slack = jnp.where((source_of == order[0]) | (receiver == order[0]) | (lengths[receiver] == 0), 0, jnp.maximum(slack, 0))
    passed = jax.random.randint(jax.random.fold_in(own, 4), (amount // 2,), 0, 1 << 20) % (slack + 1)
    lengths = lengths.at[source_of].add(-passed).at[receiver].add(passed)
    items = jnp.searchsorted(jnp.cumsum(lengths), jnp.arange(rows * top), side="right").astype(jnp.int32)
    grid = items.reshape(top, rows).T
    grid = grid[jax.random.permutation(jax.random.fold_in(own, 1), rows)]
    turn = jax.random.randint(jax.random.fold_in(own, 2), (rows, 1), 0, top)
    return jnp.take_along_axis(grid, (jnp.arange(top)[None, :] + turn) % top, axis=1)


def load_shares(count, total, bound, skew, full):
    loads = [(1 << 20) // math.isqrt(rank ** skew) + 1 for rank in range(1, count + 1)]
    largest = bound if full else min(bound, max(-(-total // count), total * loads[0] // sum(loads)))
    least = 1 if total - largest >= count - 1 else 0
    holding, rest = [largest] + [least] * (count - 1), total - largest - least * (count - 1)
    while rest > 0:
        candidates = [i for i in range(1, count) if holding[i] < largest] or [i for i in range(1, count) if holding[i] < bound]
        whole, left = sum([loads[i] for i in candidates]), rest
        for i in candidates:
            more = min(bound - holding[i], max(1, left * loads[i] // whole), rest)
            holding[i] = holding[i] + more
            rest = rest - more
    return np.array(holding)


def centred(key, shape, spread, bound, shards=(), held_as=jnp.bfloat16):
    factor_of = block_levels(key, shape, shards, -0.22, 0.18) if shards else 1.0
    array = jax.random.normal(key, shape, jnp.float32) * spread * factor_of
    return jnp.minimum(jnp.maximum(array, -bound), bound).astype(held_as)


def gaussian_with(own_key, shape, scale, reach, pieces, heavy, held_as=jnp.bfloat16):
    result = scale * jax.random.normal(own_key, shape, jnp.float32)
    if pieces:
        result = result * block_levels(own_key, shape, pieces, -0.22, 0.18)
    return jnp.clip(strengthened(result, jax.random.fold_in(own_key, 3), *heavy), -reach, reach).astype(held_as)


def setup_inputs(seed: int = 0) -> dict:
    key_list = jax.random.split(jax.random.key(seed), 14)
    moe_cotangent = centred(key_list[0], (LENGTH, D), 1.0, 6.0, ((0, 512),))
    route_ids_keys = jax.random.split(jax.random.fold_in(key_list[1], 1), LENGTH // MTOK)
    route_ids_turns = jax.random.permutation(jax.random.fold_in(key_list[1], 3), LENGTH // MTOK)
    route_ids = jax.vmap(lambda own, number: deal_out(jax.random.fold_in(key_list[1], 2), own, number, MTOK, EXPERTS, TOP, CAP, 2))(route_ids_keys, route_ids_turns).reshape((LENGTH, TOP))
    route_weights = jnp.clip(0.099609375 + 0.7988281 * jax.random.uniform(key_list[2], (LENGTH, TOP), jnp.float32) ** block_levels(key_list[2], (LENGTH, TOP), ((0, 512),), -0.2, 0.2), 0.099609375, 0.8984375).astype(jnp.bfloat16)
    saved_pre = gaussian_with(key_list[3], (EXPERTS, ROWS, FF), 1.5, 24.0, ((0, 8), (2, 64)), (2, 1, 64, 4.0))
    w_down = centred(key_list[4], (EXPERTS, FF, D), FF ** -0.5, 0.0546875, ((0, 8), (1, 64)))
    inputs = centred(key_list[5], (LENGTH, MCH), 1.0, 6.0, ((0, 16), (1, 32)))
    deltas = jnp.clip(jnp.exp(math.log(2.0) - 2.0794415 * jax.random.uniform(key_list[6], (LENGTH, MCH), jnp.float32) ** block_levels(key_list[6], (LENGTH, MCH), ((0, 16), (1, 32)), -0.2, 0.2)), 0.25, 2.0).astype(jnp.bfloat16)
    mamba_cotangent = centred(key_list[7], (LENGTH, MCH), 1.0, 6.0, ((0, 16), (1, 32)))
    b_proj = centred(key_list[8], (LENGTH, NST), 1.0, 6.0, ((0, 16),), jnp.float32)
    c_proj = centred(key_list[9], (LENGTH, NST), 1.0, 6.0, ((0, 16),), jnp.float32)
    decay_rates = jnp.clip(jnp.exp(math.log(0.2) - 9.010913 * jax.random.uniform(key_list[10], (NST, MCH), jnp.float32) ** block_levels(key_list[10], (NST, MCH), ((1, 32),), -0.2, 0.2)), 2.441406286379788e-05, 0.2)
    skip_gain = jnp.clip(1.0 + 0.1 * jax.random.normal(key_list[11], (MCH,), jnp.float32), 0.5, 1.5)
    documents = draw_documents(jax.random.fold_in(key_list[13], 71), 0)
    return {"moe_cotangent": moe_cotangent, "route_ids": route_ids, "route_weights": route_weights, "saved_pre": saved_pre, "w_down": w_down, "inputs": inputs, "deltas": deltas, "mamba_cotangent": mamba_cotangent, "b_proj": b_proj, "c_proj": c_proj, "decay_rates": decay_rates, "skip_gain": skip_gain, "documents": documents}


def affine_pair(earlier, latter):
    return (latter[0] * earlier[0], latter[0] * earlier[1] + latter[1])


def silu_slope(preact):
    sigmoid = jax.nn.sigmoid(preact)
    return sigmoid * (1.0 + preact * (1.0 - sigmoid))


def slot_rows(route_block, experts, capacity):
    flat_ids = route_block.reshape(-1).astype(jnp.int32)
    onehot = (flat_ids[:, None] == jnp.arange(experts, dtype=jnp.int32)[None, :]).astype(jnp.int32)
    before = jnp.cumsum(onehot, axis=0, dtype=jnp.int32) - onehot
    position = jnp.sum(before * onehot, axis=1).astype(jnp.int32)
    return (flat_ids * capacity + position).astype(jnp.int32)


def owner_work(received, scales, preact_low, weight_down):
    preact = preact_low.astype(jnp.float32)
    hidden = jax.nn.silu(preact).astype(jnp.bfloat16)
    produced = jnp.dot(hidden, weight_down, preferred_element_type=jnp.float32)
    route_part = jnp.sum(received.astype(jnp.float32) * produced, axis=1)
    scale_column = scales.astype(jnp.float32)[:, None]
    scaled = (received.astype(jnp.float32) * scale_column).astype(jnp.bfloat16)
    weight_term = lax.dot_general(hidden, scaled, (((0,), (0,)), ((), ())), preferred_element_type=jnp.float32).astype(jnp.bfloat16)
    back = lax.dot_general(received, weight_down, (((1,), (1,)), ((), ())), preferred_element_type=jnp.float32)
    hidden_grad = scale_column * back
    pre_part = (hidden_grad * silu_slope(preact)).astype(jnp.bfloat16)
    return route_part, weight_term, pre_part


def decay_table(deltas32, rate_row, keep_mask):
    return jnp.exp(-deltas32 * rate_row[None, :]) * keep_mask[:, None]


def forward_local(decays, driving):
    return lax.associative_scan(affine_pair, (decays, driving), axis=0)


def backward_local(decays, source):
    shifted = jnp.concatenate([decays[1:], jnp.ones_like(decays[:1])], axis=0)
    return lax.associative_scan(affine_pair, (shifted, source), axis=0, reverse=True)


def state_pass(inputs32, deltas32, cot32, b_column, c_column, rate_row, keep_mask, state_in, adjoint_in):
    decays = decay_table(deltas32, rate_row, keep_mask)
    cumulative, state_local = forward_local(decays, deltas32 * b_column[:, None] * inputs32)
    remaining, adjoint_local = backward_local(decays, c_column[:, None] * cot32)
    states = state_local + cumulative * state_in[None, :]
    adjoint = adjoint_local + remaining * adjoint_in[None, :]
    previous = jnp.concatenate([state_in[None, :], states[:-1]], axis=0)
    carried = decays * previous
    input_part = deltas32 * b_column[:, None] * adjoint
    delta_part = adjoint * (b_column[:, None] * inputs32 - rate_row[None, :] * carried)
    b_part = jnp.sum(adjoint * deltas32 * inputs32, axis=1)
    c_part = jnp.sum(cot32 * states, axis=1)
    rate_part = -jnp.sum(adjoint * deltas32 * carried, axis=0)
    return input_part, delta_part, b_part, c_part, rate_part


def mamba_sweep(inputs32, deltas32, cot32, b_rows, c_rows, rates, keep_mask, states_in, adjoints_in):
    def per_state(totals, state_items):
        rate_row, b_column, c_column, state_in, adjoint_in = state_items
        input_part, delta_part, b_part, c_part, rate_part = state_pass(inputs32, deltas32, cot32, b_column, c_column, rate_row, keep_mask, state_in, adjoint_in)
        return (totals[0] + input_part, totals[1] + delta_part), (b_part, c_part, rate_part)

    blank = jnp.zeros_like(inputs32)
    sums, columns = lax.scan(per_state, (blank, blank), (rates, b_rows.T, c_rows.T, states_in, adjoints_in))
    return sums[0], sums[1], columns[0].T, columns[1].T, columns[2]


def reference(moe_cotangent, route_ids, route_weights, saved_pre, w_down, inputs, deltas, mamba_cotangent, b_proj, c_proj, decay_rates, skip_gain, documents):
    run_count = N_DP * N_SEQ
    run_rows = N_EXPERT * CAP
    id_blocks = route_ids.reshape(run_count, N_EXPERT, MTOK, TOP)
    target = jax.vmap(jax.vmap(lambda id_block: slot_rows(id_block, EXPERTS, CAP)))(id_blocks)
    owners = target // CAP
    slot_index = target % CAP
    run_index = jnp.arange(run_count, dtype=jnp.int32)[:, None, None]
    source_index = jnp.arange(N_EXPERT, dtype=jnp.int32)[None, :, None]
    placed = (owners * ROWS + run_index * run_rows + source_index * CAP + slot_index).reshape(-1).astype(jnp.int32)
    pair_rows = jnp.repeat(moe_cotangent, TOP, axis=0)
    received = jnp.zeros((EXPERTS * ROWS, D), jnp.bfloat16).at[placed].set(pair_rows).reshape(EXPERTS, ROWS, D)
    scales = jnp.zeros((EXPERTS * ROWS,), jnp.bfloat16).at[placed].set(route_weights.reshape(-1)).reshape(EXPERTS, ROWS)
    route_part, w_down_grad, pre_grad = lax.map(lambda packed: owner_work(*packed), (received, scales, saved_pre, w_down))
    route_grad = route_part.reshape(-1)[placed].reshape(LENGTH, TOP)

    inputs32 = inputs.astype(jnp.float32)
    deltas32 = deltas.astype(jnp.float32)
    cot32 = mamba_cotangent.astype(jnp.float32)
    earlier_docs = jnp.concatenate([documents[:1], documents[:-1]])
    keep_mask = (documents == earlier_docs).astype(jnp.float32)
    blank = jnp.zeros((NST, MCH), jnp.float32)
    input_sum, delta_sum, b_grad, c_grad, rate_grad = mamba_sweep(inputs32, deltas32, cot32, b_proj, c_proj, decay_rates, keep_mask, blank, blank)
    input_grad = (input_sum + skip_gain[None, :] * cot32).astype(jnp.bfloat16)
    delta_grad = delta_sum.astype(jnp.bfloat16)
    skip_grad = jnp.sum(cot32 * inputs32, axis=0)
    return w_down_grad, route_grad, pre_grad, input_grad, delta_grad, b_grad, c_grad, rate_grad, skip_grad
```

```python
import functools

import jax
import jax.numpy as jnp
from jax import lax
from jax.experimental import pallas as pl
from jax.experimental.pallas import tpu as pltpu
from jax.sharding import PartitionSpec as P

F32, BF16 = jnp.float32, jnp.bfloat16
MESH = pl.DeviceIdType.MESH
NDP, NSEQ, NEX = 4, 16, 8
D, HID, NST, CH, TOK = 4096, 192, 16, 256, 256
LANE = 128
WIDE = D + LANE
CA = 12 * LANE
CB = CA + 11 * LANE
CHUNKS, STEPS = 8, TOK // 8
GROUP = 4
BIG = 1e9


def get2(ref, rows):
    return jnp.concatenate([ref[0, rows, :], ref[1, rows, :]], axis=1)


def put2(ref, rows, value):
    ref[0, rows, :] = value[:, 0:LANE]
    ref[1, rows, :] = value[:, LANE:CH]


def kernel(
    cot_ref, ids_ref, wts_ref, pre_ref, w_ref, x_ref, d_ref, mc_ref, b_ref, c_ref, rate_ref,
    skip_ref, doc_ref,
    wgrad_ref, route_ref, pregrad_ref, ingrad_ref, dgrad_ref, bc_ref, rategrad_ref, skipgrad_ref,
    g, asend, arecv, asm, hid_t,
    docs, bc2d, dm2, dx2, ct2, dm, dx, ct, bx, cx, dec, car, g1, g2,
    ssum, wsum, sin2, win2, summ, gath, ret, back, sbuf, wbuf,
    bcl, bc1, bc2, bc3, rs, rsr, rgg, rp, rr1, rr2, rr3,
    ssem, rsem,
):
    y, z, e = lax.axis_index("dp"), lax.axis_index("seq"), lax.axis_index("expert")
    counter = [0]
    sent = []

    def at_seq(k):
        return lax.rem(z + k + 2 * NSEQ, NSEQ)

    def at_dp(k):
        return lax.rem(y + k + 2 * NDP, NDP)

    def at_ex(k):
        return lax.rem(e + k + 2 * NEX, NEX)

    def channel():
        counter[0] += 1
        return counter[0] - 1

    def start(src, dst, slot, device):
        copy = pltpu.make_async_remote_copy(
            src_ref=src, dst_ref=dst, send_sem=ssem.at[slot], recv_sem=rsem.at[slot],
            device_id=device, device_id_type=MESH,
        )
        copy.start()
        sent.append(copy)

    def arrive(dst, slot, device):
        pltpu.make_async_remote_copy(
            src_ref=dst, dst_ref=dst, send_sem=ssem.at[slot], recv_sem=rsem.at[slot],
            device_id=device, device_id_type=MESH,
        ).wait_recv()

    barrier = pltpu.get_barrier_semaphore()
    peers = [{"seq": at_seq(k)} for k in range(1, NSEQ)]
    peers += [{"dp": at_dp(k)} for k in range(1, NDP)]
    peers += [{"expert": at_ex(k)} for k in range(1, NEX)]
    for peer in peers:
        pl.semaphore_signal(barrier, inc=1, device_id=peer, device_id_type=MESH)

    lane8 = lax.broadcasted_iota(jnp.int32, (8, LANE), 1)
    sub8 = lax.broadcasted_iota(jnp.int32, (8, LANE), 0)
    first_id, second_id = ids_ref[:, 0:1], ids_ref[:, 1:2]
    named_first = (lane8 == first_id).astype(F32)
    named_second = (lane8 == second_id).astype(F32)
    named = jnp.maximum(named_first, named_second)
    before = jnp.zeros((8, LANE), F32)
    for t in range(7):
        before += jnp.where(sub8 > t, named[t : t + 1, :], 0.0)
    slot_of = [
        jnp.where(before == float(c), named, 0.0) for c in range(2)
    ]
    weights = wts_ref[...].astype(F32)
    pair_weight = named_first * weights[:, 0:1] + named_second * weights[:, 1:2]
    rows32 = cot_ref[...].astype(F32)
    for x in range(NEX):
        for c in range(2):
            chosen = slot_of[c][:, x : x + 1]
            asend[x, c : c + 1, 0:D] = jnp.sum(chosen * rows32, axis=0, keepdims=True)
            share = jnp.sum(
                (slot_of[c] * pair_weight)[:, x : x + 1] * jnp.ones((8, LANE), F32),
                axis=0, keepdims=True,
            )
            asend[x, c : c + 1, D:WIDE] = share

    pl.semaphore_wait(barrier, len(peers))

    a2a = [channel() for _ in range(1, NEX)]
    for k in range(1, NEX):
        start(asend.at[at_ex(k)], arecv.at[e], a2a[k - 1], {"expert": at_ex(k)})
    arecv[e] = asend[e]

    def prepare():
        doc = jnp.broadcast_to(doc_ref[...].astype(F32), (TOK, LANE))
        docs[8 : TOK + 8, :] = doc
        docs[7:8, :] = doc[0:1, :]
        keep = docs[7 : TOK + 7, :] == doc
        for h in range(2):
            cols = slice(h * LANE, (h + 1) * LANE)
            d32 = d_ref[:, cols].astype(F32)
            dm2[h] = jnp.where(keep, d32, BIG)
            dx2[h] = d32 * x_ref[:, cols].astype(F32)
            ct2[h] = mc_ref[:, cols].astype(F32)
        bc2d[0, :, 0:NST] = b_ref[...]
        bc2d[1, :, 0:NST] = c_ref[...]

    def spread():
        def body(step, _):
            rows = pl.ds(step, CHUNKS, stride=STEPS)
            dm[step] = get2(dm2, rows)
            dx[step] = get2(dx2, rows)
            ct[step] = get2(ct2, rows)
            b8, c8 = bc2d[0, rows, :], bc2d[1, rows, :]
            for n in range(NST):
                bx[step, n] = jnp.broadcast_to(b8[:, n : n + 1], (8, LANE))
                cx[step, n] = jnp.broadcast_to(c8[:, n : n + 1], (8, LANE))
            return 0

        lax.fori_loop(0, STEPS, body, 0)

    def twice(v):
        return jnp.concatenate([v, v], axis=1)

    def rate_of(n):
        return jnp.broadcast_to(rate_ref[n : n + 1, :], (8, CH)) * -1.4426950408889634

    def first_forward(group):
        names = [group * GROUP + i for i in range(GROUP)]
        scale = [rate_of(n) for n in names]

        def body(it, carry):
            carry = list(carry)
            for u in range(2):
                step = it * 2 + u
                d_now, x_now = dm[step], dx[step]
                for i, n in enumerate(names):
                    decay = jnp.exp2(d_now * scale[i])
                    dec[n, step] = decay
                    carry[i] = decay * carry[i] + twice(bx[step, n]) * x_now
            return tuple(carry)

        out = lax.fori_loop(0, STEPS // 2, body, tuple(jnp.zeros((8, CH), F32) for _ in names))
        for i, n in enumerate(names):
            put2(ssum, slice(8 * n, 8 * n + 8), out[i])

    def first_backward(group):
        names = [group * GROUP + i for i in range(GROUP)]

        def body(it, carry):
            carry = list(carry)
            for u in range(2):
                step = STEPS - 1 - (it * 2 + u)
                c_now = ct[step]
                for i, n in enumerate(names):
                    carry[i] = dec[n, step] * (twice(cx[step, n]) * c_now + carry[i])
            return tuple(carry)

        out = lax.fori_loop(0, STEPS // 2, body, tuple(jnp.zeros((8, CH), F32) for _ in names))
        for i, n in enumerate(names):
            put2(wsum, slice(8 * n, 8 * n + 8), out[i])

    through = []

    def chunk_rows(k):
        return pl.ds(k, NST, stride=CHUNKS)

    def summarize():
        total = jnp.zeros((8, CH), F32)
        total = lax.fori_loop(0, STEPS, lambda s, acc: acc + dm[s], total)
        scale = rate_ref[...] * -1.4426950408889634
        for k in range(CHUNKS):
            through.append(jnp.exp2(scale * total[k : k + 1, :]))
        state = jnp.zeros((NST, CH), F32)
        whole = jnp.ones((NST, CH), F32)
        for k in range(CHUNKS):
            state = get2(ssum, chunk_rows(k)) + through[k] * state
            whole = whole * through[k]
        adjoint = jnp.zeros((NST, CH), F32)
        for k in reversed(range(CHUNKS)):
            adjoint = get2(wsum, chunk_rows(k)) + through[k] * adjoint
        ends = jnp.concatenate([docs[8:9, :], docs[TOK + 7 : TOK + 8, :]], axis=1)
        for n in range(NST):
            summ[n, 0:1, :] = whole[n : n + 1, :]
            summ[n, 1:2, :] = state[n : n + 1, :]
            summ[n, 2:3, :] = adjoint[n : n + 1, :]
            summ[n, 3:4, :] = ends
        slots = [channel() for _ in range(1, NSEQ)]
        for k in range(1, NSEQ):
            start(summ.at[at_seq(k)], gath.at[z], slots[k - 1], {"seq": at_seq(k)})
        gath[z] = summ[z]
        return slots

    def carry_over(slots):
        for k in range(1, NSEQ):
            arrive(gath.at[at_seq(-k)], slots[k - 1], {"seq": at_seq(-k)})
        same = [jnp.zeros((1, CH), F32)]
        for p in range(1, NSEQ):
            here = gath[p, 3:4, 0:LANE]
            there = gath[p - 1, 3:4, LANE:CH]
            same.append(twice((here == there).astype(F32)))
        same.append(jnp.zeros((1, CH), F32))
        state = jnp.zeros((1, CH), F32)
        for p in range(NSEQ):
            entering = same[p] * state
            ret[p, 0:1, :] = entering
            state = gath[p, 1:2, :] + gath[p, 0:1, :] * entering
        adjoint = jnp.zeros((1, CH), F32)
        for p in reversed(range(NSEQ)):
            entering = same[p + 1] * adjoint
            ret[p, 1:2, :] = entering
            adjoint = gath[p, 2:3, :] + gath[p, 0:1, :] * entering
        slots = [channel() for _ in range(1, NSEQ)]
        for k in range(1, NSEQ):
            start(ret.at[at_seq(k)], back.at[z], slots[k - 1], {"seq": at_seq(k)})
        back[z] = ret[z]
        return slots

    def enter(slots):
        for k in range(1, NSEQ):
            arrive(back.at[at_seq(-k)], slots[k - 1], {"seq": at_seq(-k)})
        for n in range(NST):
            sbuf[n : n + 1, :] = back[n, 0:1, :]
            wbuf[n : n + 1, :] = back[n, 1:2, :]
        state = sbuf[...]
        for k in range(CHUNKS):
            put2(sin2, chunk_rows(k), state)
            state = get2(ssum, chunk_rows(k)) + through[k] * state
        adjoint = wbuf[...]
        for k in reversed(range(CHUNKS)):
            put2(win2, chunk_rows(k), adjoint)
            adjoint = get2(wsum, chunk_rows(k)) + through[k] * adjoint

    def placed(total, column, position):
        return jnp.where(lane8 == position, column, total)

    def lanes_sum(v):
        return jnp.sum(v[:, 0:LANE] + v[:, LANE:CH], axis=1, keepdims=True)

    def second_forward(group):
        names = [group * GROUP + i for i in range(GROUP)]

        def body(it, carry):
            states, sums = list(carry[:GROUP]), list(carry[GROUP:])
            for u in range(2):
                step = it * 2 + u
                x_now, c_now = dx[step], ct[step]
                for i, n in enumerate(names):
                    carried = dec[n, step] * states[i]
                    car[n, step] = carried
                    states[i] = carried + twice(bx[step, n]) * x_now
                    column = lanes_sum(states[i] * c_now)
                    sums[i // 2] = placed(sums[i // 2], column, step + (64 * (i % 2) + 32))
            return tuple(states + sums)

        init = [get2(sin2, slice(8 * n, 8 * n + 8)) for n in names]
        init += [jnp.zeros((8, LANE), F32)] * (GROUP // 2)
        out = lax.fori_loop(0, STEPS // 2, body, tuple(init))
        for i in range(GROUP // 2):
            bcl[group * (GROUP // 2) + i] = out[GROUP + i]

    def second_backward(group):
        names = [group * GROUP + i for i in range(GROUP)]
        rates = [jnp.broadcast_to(rate_ref[n : n + 1, :], (8, CH)) for n in names]

        def body(it, carry):
            adj = list(carry[:GROUP])
            grads = list(carry[GROUP : 2 * GROUP])
            sums = list(carry[2 * GROUP :])
            for u in range(2):
                step = STEPS - 1 - (it * 2 + u)
                d_now, x_now, c_now = dm[step], dx[step], ct[step]
                rows = pl.ds(pl.multiple_of(step * 8, 8), 8)
                if group == 0:
                    sum1 = sum2 = jnp.zeros((8, CH), F32)
                else:
                    sum1, sum2 = get2(g1, rows), get2(g2, rows)
                for i, n in enumerate(names):
                    here = twice(cx[step, n]) * c_now + adj[i]
                    adj[i] = dec[n, step] * here
                    product = here * car[n, step]
                    sum1 = sum1 + twice(bx[step, n]) * here
                    sum2 = sum2 + rates[i] * product
                    grads[i] = grads[i] + d_now * product
                    column = lanes_sum(here * x_now)
                    sums[i // 2] = placed(sums[i // 2], column, step + 64 * (i % 2))
                put2(g1, rows, sum1)
                put2(g2, rows, sum2)
            return tuple(adj + grads + sums)

        init = [get2(win2, slice(8 * n, 8 * n + 8)) for n in names]
        init += [jnp.zeros((8, CH), F32)] * GROUP
        init += [bcl[group * (GROUP // 2) + i] for i in range(GROUP // 2)]
        out = lax.fori_loop(0, STEPS // 2, body, tuple(init))
        for i, n in enumerate(names):
            rs[n, 0:1, :] = -jnp.sum(out[GROUP + i], axis=0, keepdims=True)
        for i in range(GROUP // 2):
            bcl[group * (GROUP // 2) + i] = out[2 * GROUP + i]

    def first_sums():
        skip = jnp.sum(mc_ref[...].astype(F32) * x_ref[...].astype(F32), axis=0, keepdims=True)
        for n in range(NST):
            rs[n, 1:2, :] = skip
        by_seq = [channel() for _ in range(1, NSEQ)]
        by_ex = [channel() for _ in range(1, NEX)]
        for k in range(1, NEX):
            start(bcl.at[at_ex(k)], bc1.at[e], by_ex[k - 1], {"expert": at_ex(k)})
        for k in range(1, NSEQ):
            start(rs.at[at_seq(k)], rsr.at[z], by_seq[k - 1], {"seq": at_seq(k)})
        bc1[e] = bcl[e]
        rsr[z] = rs[z]
        return by_seq, by_ex

    def second_sums(slots):
        by_seq, by_ex = slots
        for k in range(1, NEX):
            arrive(bc1.at[at_ex(-k)], by_ex[k - 1], {"expert": at_ex(-k)})
        tile = bc1[0]
        for k in range(1, NEX):
            tile = tile + bc1[k]
        bc2[y] = tile
        by_dp = [channel() for _ in range(1, NDP)]
        for k in range(1, NDP):
            start(bc2.at[y], bc2.at[y], by_dp[k - 1], {"dp": at_dp(k)})
        for k in range(1, NSEQ):
            arrive(rsr.at[at_seq(-k)], by_seq[k - 1], {"seq": at_seq(-k)})
        total = rsr[0]
        for p in range(1, NSEQ):
            total = total + rsr[p]
        skipgrad_ref[...] = total[1:2, :]
        rgg[z] = total[0:1, :]
        by_seq = [channel() for _ in range(1, NSEQ)]
        for k in range(1, NSEQ):
            start(rgg.at[z], rgg.at[z], by_seq[k - 1], {"seq": at_seq(k)})
        return by_seq, by_dp

    def third_sums(slots):
        by_seq, by_dp = slots
        for k in range(1, NDP):
            arrive(bc2.at[at_dp(-k)], by_dp[k - 1], {"dp": at_dp(-k)})
        bc3[e] = ((bc2[0] + bc2[1]) + bc2[2]) + bc2[3]
        by_ex = [channel() for _ in range(1, NEX)]
        for k in range(1, NEX):
            start(bc3.at[e], bc3.at[e], by_ex[k - 1], {"expert": at_ex(k)})
        return by_seq, by_ex

    def last_sums(slots):
        by_seq, by_ex = slots
        for k in range(1, NSEQ):
            arrive(rgg.at[at_seq(-k)], by_seq[k - 1], {"seq": at_seq(-k)})
        for n in range(NST):
            rategrad_ref[n : n + 1, :] = rgg[n]
        for k in range(1, NEX):
            arrive(bc3.at[at_ex(-k)], by_ex[k - 1], {"expert": at_ex(-k)})
        bc_ref[...] = bc3[...]

    def finish_scan():
        for k in range(CHUNKS):
            rows = slice(k * STEPS, (k + 1) * STEPS)
            ours = pl.ds(k, STEPS, stride=CHUNKS)
            sum1, sum2 = get2(g1, ours), get2(g2, ours)
            into = d_ref[rows, :].astype(F32) * sum1 + skip_ref[...] * mc_ref[rows, :].astype(F32)
            ingrad_ref[rows, :] = into.astype(BF16)
            dgrad_ref[rows, :] = (x_ref[rows, :].astype(F32) * sum1 - sum2).astype(BF16)

    def ring_item(name, seq, where=None):
        if name == "b":
            return g.at[y, seq, :, CA:WIDE]
        if name == "b1":
            return g.at[y, seq, :, CA:CB]
        if name == "b2":
            return g.at[y, seq, :, CB:WIDE]
        if name == "a1":
            return g.at[0:2, seq, :, 0:CA]
        return g.at[2:4, seq, :, 0:CA]

    def gather():
        plus, minus = {"seq": at_seq(1)}, {"seq": at_seq(-1)}
        up, down = {"dp": at_dp(1)}, {"dp": at_dp(-1)}
        ring = {}

        def ring_send(name, step, sign):
            seq = at_seq(-sign * (step - 1))
            ring[name, step, sign] = channel()
            start(ring_item(name, seq), ring_item(name, seq), ring[name, step, sign],
                  plus if sign > 0 else minus)

        def ring_wait(name, step, sign):
            arrive(ring_item(name, at_seq(-sign * step)), ring[name, step, sign],
                   minus if sign > 0 else plus)

        across = {}

        def across_send(dist):
            seq = at_seq(dist)
            across[dist] = [channel() for _ in range(4)]
            part = g.at[y, seq, :, CA:WIDE]
            start(part, part, across[dist][0], up)
            start(part, part, across[dist][1], down)

        def across_pass(dist):
            seq = at_seq(dist)
            slots = across[dist]
            arrive(g.at[at_dp(-1), seq, :, CA:WIDE], slots[0], down)
            half = g.at[at_dp(-1), seq, :, CA:CB]
            start(half, half, slots[2], up)
            arrive(g.at[at_dp(1), seq, :, CA:WIDE], slots[1], up)
            half = g.at[at_dp(1), seq, :, CB:WIDE]
            start(half, half, slots[3], down)

        def across_end(dist):
            seq = at_seq(dist)
            slots = across[dist]
            arrive(g.at[at_dp(2), seq, :, CA:CB], slots[2], down)
            arrive(g.at[at_dp(2), seq, :, CB:WIDE], slots[3], up)

        first = [channel() for _ in range(1, NDP)]
        mine = g.at[y, z, :, 0:CA]
        for k in range(1, NDP):
            start(mine, mine, first[k - 1], {"dp": at_dp(k)})
        ring_send("b", 1, 1)
        ring_send("b", 1, -1)
        across_send(0)
        yield
        for k in range(1, NDP):
            arrive(g.at[at_dp(-k), z, :, 0:CA], first[k - 1], {"dp": at_dp(-k)})
        for name in ("a1", "a2"):
            ring_send(name, 1, 1)
            ring_send(name, 1, -1)
        yield
        half = NSEQ // 2
        pending = [0]
        for step in range(1, half):
            for name in ("b", "a1", "a2"):
                for sign in (1, -1):
                    ring_wait(name, step, sign)
                    if step < half - 1:
                        ring_send(name, step + 1, sign)
                    elif name == "b":
                        ring_send("b1" if sign > 0 else "b2", half, sign)
                    elif (name == "a1") == (sign > 0):
                        ring_send(name, half, sign)
                if name == "b":
                    across_send(-step)
                    across_send(step)
                    for dist in pending:
                        across_pass(dist)
                    ended, pending = pending, [-step, step]
                yield
            for dist in ended:
                across_end(dist)
        ring_wait("b1", half, 1)
        ring_wait("b2", half, -1)
        across_send(half)
        yield
        for dist in pending:
            across_pass(dist)
        yield
        across_pass(half)
        ring_wait("a1", half, 1)
        ring_wait("a2", half, -1)
        for dist in pending + [half]:
            across_end(dist)

    def hidden_block(block):
        pre = pre_ref[block].reshape(256, HID).astype(F32)
        hidden = (pre * jax.nn.sigmoid(pre)).astype(BF16)
        hid_t[:, 256 * block : 256 * block + 256] = hidden.astype(F32).T.astype(BF16)

    def back_block(block, _):
        seqs = pl.ds(block * 4, 4)
        rows = g[:, seqs, :, 0:D].reshape(256, D)
        product = lax.dot_general(
            rows, w_ref[...], (((1,), (1,)), ((), ())), preferred_element_type=F32
        )
        scale = g[:, seqs, :, D:WIDE].reshape(256, LANE).astype(F32)
        scale = jnp.concatenate([scale, scale[:, 0 : HID - LANE]], axis=1)
        pre = pre_ref[:, seqs].reshape(256, HID).astype(F32)
        sig = jax.nn.sigmoid(pre)
        hidden = (pre * sig).astype(BF16).astype(F32)
        slope = sig * (1.0 + pre * (1.0 - sig))
        pregrad_ref[:, seqs] = ((scale * product) * slope).astype(BF16).reshape(4, 4, 16, HID)
        column = jnp.sum(hidden * product, axis=1, keepdims=True)
        eye = lax.broadcasted_iota(jnp.int32, (LANE, LANE), 0) == lax.broadcasted_iota(
            jnp.int32, (LANE, LANE), 1
        )
        for h in range(2):
            part = column[h * LANE : (h + 1) * LANE, :]
            rp[block, h : h + 1, :] = jnp.sum(jnp.where(eye, part, 0.0), axis=0, keepdims=True)
        return 0

    def weight_tile(tile, _):
        width = 512
        cols = pl.ds(pl.multiple_of(tile * width, width), width)
        scale = g[:, :, :, D:WIDE].reshape(1024, LANE).astype(F32)
        scale = jnp.concatenate([scale] * (width // LANE), axis=1)
        rows = g[:, :, :, cols].reshape(1024, width).astype(F32)
        scaled = (rows * scale).astype(BF16)
        wgrad_ref[:, cols] = jnp.dot(
            hid_t[...], scaled, preferred_element_type=F32
        ).astype(BF16)
        return 0

    prepare()
    for k in range(1, NEX):
        arrive(arecv.at[at_ex(-k)], a2a[k - 1], {"expert": at_ex(-k)})
    for q in range(NEX):
        asm[2 * q : 2 * q + 2, :] = arecv[q]
    g[y, z] = asm[...].astype(BF16)

    gathering = gather()
    tick = functools.partial(next, gathering, None)
    tick()
    spread()
    tick()
    for group in range(NST // GROUP):
        first_forward(group)
        first_backward(group)
        tick()
    slots = summarize()
    tick()
    hidden_block(0)
    hidden_block(1)
    tick()
    slots = carry_over(slots)
    tick()
    hidden_block(2)
    hidden_block(3)
    tick()
    enter(slots)
    for group in range(NST // GROUP):
        tick()
        second_forward(group)
    for group in range(NST // GROUP):
        tick()
        second_backward(group)
    tick()
    slots = first_sums()
    finish_scan()
    tick()
    slots = second_sums(slots)
    tick()
    slots = third_sums(slots)
    tick()
    last_sums(slots)
    for _ in gathering:
        pass

    lax.fori_loop(0, 4, back_block, 0)
    by_seq = [channel() for _ in range(1, NSEQ)]
    for k in range(1, NSEQ):
        start(rp.at[at_seq(k) // 4], rr1.at[z], by_seq[k - 1], {"seq": at_seq(k)})
    rr1[z] = rp[z // 4]
    lax.fori_loop(0, 4, weight_tile, 0)
    for k in range(1, NSEQ):
        arrive(rr1.at[at_seq(-k)], by_seq[k - 1], {"seq": at_seq(-k)})
    total = rr1[0]
    for p in range(1, NSEQ):
        total = total + rr1[p]
    rr2[y] = total
    by_dp = [channel() for _ in range(1, NDP)]
    for k in range(1, NDP):
        start(rr2.at[y], rr2.at[y], by_dp[k - 1], {"dp": at_dp(k)})
    lax.fori_loop(4, 6, weight_tile, 0)
    for k in range(1, NDP):
        arrive(rr2.at[at_dp(-k)], by_dp[k - 1], {"dp": at_dp(-k)})
    rr3[e] = ((rr2[0] + rr2[1]) + rr2[2]) + rr2[3]
    by_ex = [channel() for _ in range(1, NEX)]
    for k in range(1, NEX):
        start(rr3.at[e], rr3.at[e], by_ex[k - 1], {"expert": at_ex(k)})
    lax.fori_loop(6, 8, weight_tile, 0)
    for k in range(1, NEX):
        arrive(rr3.at[at_ex(-k)], by_ex[k - 1], {"expert": at_ex(-k)})

    row_of = lax.broadcasted_iota(jnp.int32, (2, LANE), 0)
    lane_of = lax.broadcasted_iota(jnp.int32, (2, LANE), 1)
    base = (y % 2) * 64 + (z % 4) * 16 + e * 2
    picked = jnp.zeros((8, LANE), F32)
    for c in range(2):
        values = jnp.zeros((1, LANE), F32)
        for x in range(NEX):
            here = (row_of == y // 2) & (lane_of == base + c)
            value = jnp.sum(
                jnp.sum(jnp.where(here, rr3[x], 0.0), axis=0, keepdims=True),
                axis=1, keepdims=True,
            )
            values = jnp.where(lane8[0:1, :] == x, value, values)
        picked = picked + slot_of[c] * values
    route_first = jnp.sum(picked * named_first, axis=1, keepdims=True)
    route_second = jnp.sum(picked * named_second, axis=1, keepdims=True)
    route_ref[...] = jnp.where(lane8 == 0, route_first, route_second)[:, 0:2]

    for copy in sent:
        copy.wait_send()


def local(
    moe_cotangent, route_ids, route_weights, saved_pre, w_down, inputs, deltas, mamba_cotangent,
    b_proj, c_proj, decay_rates, skip_gain, documents,
):
    vmem = pl.BlockSpec(memory_space=pltpu.VMEM)

    def out(shape, dtype):
        return jax.ShapeDtypeStruct(shape, dtype)

    def f32(*shape):
        return pltpu.VMEM(shape, F32)

    copies = 320
    wgrad, route, pregrad, ingrad, dgrad, bc, rategrad, skipgrad = pl.pallas_call(
        kernel,
        out_shape=(
            out((HID, D), BF16),
            out((8, 2), F32),
            out((NDP, NSEQ, 16, HID), BF16),
            out((TOK, CH), BF16),
            out((TOK, CH), BF16),
            out((8, 8, LANE), F32),
            out((NST, CH), F32),
            out((1, CH), F32),
        ),
        in_specs=[vmem] * 13,
        out_specs=[vmem] * 8,
        scratch_shapes=[
            pltpu.VMEM((NDP, NSEQ, 16, WIDE), BF16),
            f32(NEX, 2, WIDE), f32(NEX, 2, WIDE), f32(16, WIDE),
            pltpu.VMEM((HID, 1024), BF16),
            f32(TOK + 8, LANE),
            f32(2, TOK, LANE), f32(2, TOK, LANE), f32(2, TOK, LANE), f32(2, TOK, LANE),
            f32(STEPS, 8, CH), f32(STEPS, 8, CH), f32(STEPS, 8, CH),
            f32(STEPS, NST, 8, LANE), f32(STEPS, NST, 8, LANE),
            f32(NST, STEPS, 8, CH), f32(NST, STEPS, 8, CH),
            f32(2, TOK, LANE), f32(2, TOK, LANE),
            f32(2, TOK // 2, LANE), f32(2, TOK // 2, LANE),
            f32(2, TOK // 2, LANE), f32(2, TOK // 2, LANE),
            f32(NST, 4, CH), f32(NSEQ, 4, CH), f32(NSEQ, 2, CH), f32(NST, 2, CH),
            f32(NST, CH), f32(NST, CH),
            f32(8, 8, LANE), f32(8, 8, LANE), f32(NDP, 8, LANE), f32(8, 8, LANE),
            f32(NST, 2, CH), f32(NSEQ, 2, CH), f32(NST, 1, CH),
            f32(4, 2, LANE), f32(NSEQ, 2, LANE), f32(NDP, 2, LANE), f32(NEX, 2, LANE),
            pltpu.SemaphoreType.DMA((copies,)),
            pltpu.SemaphoreType.DMA((copies,)),
        ],
        compiler_params=pltpu.CompilerParams(
            collective_id=0, has_side_effects=True, vmem_limit_bytes=56 * 1024 * 1024
        ),
    )(
        moe_cotangent, route_ids, route_weights,
        saved_pre.reshape(NDP, NSEQ, 16, HID), w_down.reshape(HID, D),
        inputs, deltas, mamba_cotangent, b_proj, c_proj, decay_rates,
        skip_gain.reshape(1, CH), documents.reshape(TOK, 1),
    )
    both = bc.reshape(8, CHUNKS, 2, 2, STEPS).transpose(3, 1, 4, 0, 2).reshape(2, TOK, NST)
    return (
        wgrad.reshape(1, HID, D),
        route,
        pregrad.reshape(1, 1024, HID),
        ingrad,
        dgrad,
        both[0],
        both[1],
        rategrad,
        skipgrad.reshape(CH),
    )


def solution(mesh):
    return jax.shard_map(
        local,
        mesh=mesh,
        in_specs=(
            P(("dp", "seq", "expert"), None),
            P(("dp", "seq", "expert"), None),
            P(("dp", "seq", "expert"), None),
            P("expert", None, ("dp", "seq")),
            P("expert", ("dp", "seq"), None),
            P("seq", ("dp", "expert")),
            P("seq", ("dp", "expert")),
            P("seq", ("dp", "expert")),
            P("seq", None),
            P("seq", None),
            P(None, ("dp", "expert")),
            P(("dp", "expert")),
            P("seq"),
        ),
        out_specs=(
            P("expert", ("dp", "seq"), None),
            P(("dp", "seq", "expert"), None),
            P("expert", None, ("dp", "seq")),
            P("seq", ("dp", "expert")),
            P("seq", ("dp", "expert")),
            P("seq", None),
            P("seq", None),
            P(None, ("dp", "expert")),
            P(("dp", "expert")),
        ),
        check_vma=False,
    )
```

```python
import functools

import jax
import jax.numpy as jnp
from jax import lax
from jax.experimental import pallas as pl
from jax.experimental.pallas import tpu as pltpu
from jax.sharding import PartitionSpec as P

F32, BF16 = jnp.float32, jnp.bfloat16
MESH = pl.DeviceIdType.MESH
NDP, NSEQ, NEX = 4, 16, 8
D, HID, NST, CH, TOK = 4096, 192, 16, 256, 256
LANE = 128
WIDE = D + LANE
CA = 12 * LANE
CB = CA + 11 * LANE
CHUNKS, STEPS = 8, TOK // 8
GROUP = 4
BIG = 1e9


def get2(ref, rows):
    return jnp.concatenate([ref[0, rows, :], ref[1, rows, :]], axis=1)


def put2(ref, rows, value):
    ref[0, rows, :] = value[:, 0:LANE]
    ref[1, rows, :] = value[:, LANE:CH]


def kernel(
    cot_ref, ids_ref, wts_ref, *refs
):
    count_in, count_out = 10, 9
    far_in, refs = refs[:count_in], refs[count_in:]
    far_out, refs = refs[:count_out], refs[count_out:]
    near_in, refs = refs[:count_in], refs[count_in:]
    near_out, refs = refs[:count_out], refs[count_out:]
    pre_ref, w_ref, x_ref, d_ref, mc_ref, b_ref, c_ref, rate_ref, skip_ref, doc_ref = near_in
    (
        wgrad_ref, route_ref, pregrad_ref, ingrad_ref, dgrad_ref, bgrad_ref, cgrad_ref,
        rategrad_ref, skipgrad_ref,
    ) = near_out
    (
        g, asend, arecv, asm, hid_t, hid_r, slope_t, backs,
        docs, bc2d, dm2, dx2, ct2, dm, dx, ct, bx, cx, dec, car, g1, g2,
        ssum, wsum, sin2, win2, summ, gath, ret, back, sbuf, wbuf,
        bcl, bc1, bc2, bc3, rs, rsr, rgg, rp, rr1, rr2, rr3,
        ssem, rsem, isem, osem, tsem,
    ) = refs
    loads = [
        pltpu.make_async_copy(far, near, isem.at[i])
        for i, (far, near) in enumerate(zip(far_in, near_in))
    ]
    stores = [None] + [
        pltpu.make_async_copy(near_out[i], far_out[i], osem.at[i]) for i in range(1, count_out)
    ]

    y, z, e = lax.axis_index("dp"), lax.axis_index("seq"), lax.axis_index("expert")
    counter = [0]
    sent = []

    def at_seq(k):
        return lax.rem(z + k + 2 * NSEQ, NSEQ)

    def at_dp(k):
        return lax.rem(y + k + 2 * NDP, NDP)

    def at_ex(k):
        return lax.rem(e + k + 2 * NEX, NEX)

    def channel():
        counter[0] += 1
        return counter[0] - 1

    def start(src, dst, slot, device):
        copy = pltpu.make_async_remote_copy(
            src_ref=src, dst_ref=dst, send_sem=ssem.at[slot], recv_sem=rsem.at[slot],
            device_id=device, device_id_type=MESH,
        )
        copy.start()
        sent.append(copy)

    def arrive(dst, slot, device):
        pltpu.make_async_remote_copy(
            src_ref=dst, dst_ref=dst, send_sem=ssem.at[slot], recv_sem=rsem.at[slot],
            device_id=device, device_id_type=MESH,
        ).wait_recv()

    barrier = pltpu.get_barrier_semaphore()
    peers = [{"seq": at_seq(k)} for k in range(1, NSEQ)]
    peers += [{"dp": at_dp(k)} for k in range(1, NDP)]
    peers += [{"expert": at_ex(k)} for k in range(1, NEX)]
    for peer in peers:
        pl.semaphore_signal(barrier, inc=1, device_id=peer, device_id_type=MESH)

    for i in (2, 3, 4, 5, 6, 7, 8, 9, 0, 1):
        loads[i].start()

    lane8 = lax.broadcasted_iota(jnp.int32, (8, LANE), 1)
    sub8 = lax.broadcasted_iota(jnp.int32, (8, LANE), 0)
    eye8 = lane8[:, 0:8] == sub8[:, 0:8]

    def column(row):
        return jnp.sum(
            jnp.where(eye8, jnp.broadcast_to(row, (8, 8)), 0.0), axis=1, keepdims=True
        )

    lanes32 = lane8.astype(F32)
    named_first = (lanes32 == column(ids_ref[0:1, :].astype(F32))).astype(F32)
    named_second = (lanes32 == column(ids_ref[1:2, :].astype(F32))).astype(F32)
    named = jnp.maximum(named_first, named_second)
    before = jnp.zeros((8, LANE), F32)
    for t in range(7):
        before += jnp.where(sub8 > t, named[t : t + 1, :], 0.0)
    slot_of = [
        jnp.where(before == float(c), named, 0.0) for c in range(2)
    ]
    weights = wts_ref[...].astype(F32)
    pair_weight = named_first * column(weights[0:1, :]) + named_second * column(weights[1:2, :])
    rows32 = cot_ref[...].astype(F32)
    for x in range(NEX):
        for c in range(2):
            chosen = slot_of[c][:, x : x + 1]
            asend[x, c : c + 1, 0:D] = jnp.sum(chosen * rows32, axis=0, keepdims=True)
            share = jnp.sum(
                (slot_of[c] * pair_weight)[:, x : x + 1] * jnp.ones((8, LANE), F32),
                axis=0, keepdims=True,
            )
            asend[x, c : c + 1, D:WIDE] = share

    pl.semaphore_wait(barrier, len(peers))

    a2a = [channel() for _ in range(1, NEX)]
    for k in range(1, NEX):
        start(asend.at[at_ex(k)], arecv.at[e], a2a[k - 1], {"expert": at_ex(k)})
    arecv[e] = asend[e]

    def prepare():
        for h in range(2):
            row = doc_ref[:, h * LANE : (h + 1) * LANE].astype(F32)
            docs[8 + h * LANE : 8 + (h + 1) * LANE, :] = jnp.broadcast_to(row, (LANE, LANE)).T
        doc = docs[8 : TOK + 8, :]
        docs[7:8, :] = doc[0:1, :]
        keep = docs[7 : TOK + 7, :] == doc
        for h in range(2):
            cols = slice(h * LANE, (h + 1) * LANE)
            d32 = d_ref[:, cols].astype(F32)
            dm2[h] = jnp.where(keep, d32, BIG)
            dx2[h] = d32 * x_ref[:, cols].astype(F32)
            ct2[h] = mc_ref[:, cols].astype(F32)
            for i, ref in enumerate((b_ref, c_ref)):
                tall = [ref[:, cols], jnp.zeros((LANE - NST, LANE), F32)]
                bc2d[i, cols, :] = jnp.concatenate(tall, axis=0).T

    def spread():
        def body(step, _):
            rows = pl.ds(step, CHUNKS, stride=STEPS)
            dm[step] = get2(dm2, rows)
            dx[step] = get2(dx2, rows)
            ct[step] = get2(ct2, rows)
            b8, c8 = bc2d[0, rows, :], bc2d[1, rows, :]
            for n in range(NST):
                bx[step, n] = jnp.broadcast_to(b8[:, n : n + 1], (8, LANE))
                cx[step, n] = jnp.broadcast_to(c8[:, n : n + 1], (8, LANE))
            return 0

        lax.fori_loop(0, STEPS, body, 0)

    def twice(v):
        return jnp.concatenate([v, v], axis=1)

    def rate_of(n):
        return jnp.broadcast_to(rate_ref[n : n + 1, :], (8, CH)) * -1.4426950408889634

    def first_forward(group):
        names = [group * GROUP + i for i in range(GROUP)]
        scale = [rate_of(n) for n in names]

        def body(it, carry):
            carry = list(carry)
            for u in range(2):
                step = it * 2 + u
                d_now, x_now = dm[step], dx[step]
                for i, n in enumerate(names):
                    decay = jnp.exp2(d_now * scale[i])
                    dec[n, step] = decay
                    carry[i] = decay * carry[i] + twice(bx[step, n]) * x_now
            return tuple(carry)

        out = lax.fori_loop(0, STEPS // 2, body, tuple(jnp.zeros((8, CH), F32) for _ in names))
        for i, n in enumerate(names):
            put2(ssum, slice(8 * n, 8 * n + 8), out[i])

    def first_backward(group):
        names = [group * GROUP + i for i in range(GROUP)]

        def body(it, carry):
            carry = list(carry)
            for u in range(2):
                step = STEPS - 1 - (it * 2 + u)
                c_now = ct[step]
                for i, n in enumerate(names):
                    carry[i] = dec[n, step] * (twice(cx[step, n]) * c_now + carry[i])
            return tuple(carry)

        out = lax.fori_loop(0, STEPS // 2, body, tuple(jnp.zeros((8, CH), F32) for _ in names))
        for i, n in enumerate(names):
            put2(wsum, slice(8 * n, 8 * n + 8), out[i])

    through = []

    def chunk_rows(k):
        return pl.ds(k, NST, stride=CHUNKS)

    def summarize():
        total = jnp.zeros((8, CH), F32)
        total = lax.fori_loop(0, STEPS, lambda s, acc: acc + dm[s], total)
        scale = rate_ref[...] * -1.4426950408889634
        for k in range(CHUNKS):
            through.append(jnp.exp2(scale * total[k : k + 1, :]))
        state = jnp.zeros((NST, CH), F32)
        whole = jnp.ones((NST, CH), F32)
        for k in range(CHUNKS):
            state = get2(ssum, chunk_rows(k)) + through[k] * state
            whole = whole * through[k]
        adjoint = jnp.zeros((NST, CH), F32)
        for k in reversed(range(CHUNKS)):
            adjoint = get2(wsum, chunk_rows(k)) + through[k] * adjoint
        ends = jnp.concatenate([docs[8:9, :], docs[TOK + 7 : TOK + 8, :]], axis=1)
        for n in range(NST):
            summ[n, 0:1, :] = whole[n : n + 1, :]
            summ[n, 1:2, :] = state[n : n + 1, :]
            summ[n, 2:3, :] = adjoint[n : n + 1, :]
            summ[n, 3:4, :] = ends
        slots = [channel() for _ in range(1, NSEQ)]
        for k in range(1, NSEQ):
            start(summ.at[at_seq(k)], gath.at[z], slots[k - 1], {"seq": at_seq(k)})
        gath[z] = summ[z]
        return slots

    def carry_over(slots):
        for k in range(1, NSEQ):
            arrive(gath.at[at_seq(-k)], slots[k - 1], {"seq": at_seq(-k)})
        same = [jnp.zeros((1, CH), F32)]
        for p in range(1, NSEQ):
            here = gath[p, 3:4, 0:LANE]
            there = gath[p - 1, 3:4, LANE:CH]
            same.append(twice((here == there).astype(F32)))
        same.append(jnp.zeros((1, CH), F32))
        state = jnp.zeros((1, CH), F32)
        for p in range(NSEQ):
            entering = same[p] * state
            ret[p, 0:1, :] = entering
            state = gath[p, 1:2, :] + gath[p, 0:1, :] * entering
        adjoint = jnp.zeros((1, CH), F32)
        for p in reversed(range(NSEQ)):
            entering = same[p + 1] * adjoint
            ret[p, 1:2, :] = entering
            adjoint = gath[p, 2:3, :] + gath[p, 0:1, :] * entering
        slots = [channel() for _ in range(1, NSEQ)]
        for k in range(1, NSEQ):
            start(ret.at[at_seq(k)], back.at[z], slots[k - 1], {"seq": at_seq(k)})
        back[z] = ret[z]
        return slots

    def enter(slots):
        for k in range(1, NSEQ):
            arrive(back.at[at_seq(-k)], slots[k - 1], {"seq": at_seq(-k)})
        for n in range(NST):
            sbuf[n : n + 1, :] = back[n, 0:1, :]
            wbuf[n : n + 1, :] = back[n, 1:2, :]
        state = sbuf[...]
        for k in range(CHUNKS):
            put2(sin2, chunk_rows(k), state)
            state = get2(ssum, chunk_rows(k)) + through[k] * state
        adjoint = wbuf[...]
        for k in reversed(range(CHUNKS)):
            put2(win2, chunk_rows(k), adjoint)
            adjoint = get2(wsum, chunk_rows(k)) + through[k] * adjoint

    place = (sub8 % 4) * STEPS

    def in_rows(n, first, value):
        at = first + 2 * (n % 2)
        bcl[n // 2, at : at + 1, :] = jnp.sum(value[0:4, :], axis=0, keepdims=True)
        bcl[n // 2, at + 1 : at + 2, :] = jnp.sum(value[4:8, :], axis=0, keepdims=True)

    def lanes_sum(v):
        return jnp.sum(v[:, 0:LANE] + v[:, LANE:CH], axis=1, keepdims=True)

    def second_forward(group):
        names = [group * GROUP + i for i in range(GROUP)]

        def body(it, carry):
            states, sums = list(carry[:GROUP]), list(carry[GROUP:])
            for u in range(2):
                step = it * 2 + u
                x_now, c_now = dx[step], ct[step]
                here = lane8 == place + step
                for i, n in enumerate(names):
                    carried = dec[n, step] * states[i]
                    car[n, step] = carried
                    states[i] = carried + twice(bx[step, n]) * x_now
                    total = lanes_sum(states[i] * c_now)
                    sums[i] = jnp.where(here, total, sums[i])
            return tuple(states + sums)

        init = [get2(sin2, slice(8 * n, 8 * n + 8)) for n in names]
        init += [jnp.zeros((8, LANE), F32)] * GROUP
        out = lax.fori_loop(0, STEPS // 2, body, tuple(init))
        for i, n in enumerate(names):
            in_rows(n, 4, out[GROUP + i])

    def second_backward(group):
        names = [group * GROUP + i for i in range(GROUP)]
        rates = [jnp.broadcast_to(rate_ref[n : n + 1, :], (8, CH)) for n in names]

        def body(it, carry):
            adj = list(carry[:GROUP])
            grads = list(carry[GROUP : 2 * GROUP])
            sums = list(carry[2 * GROUP :])
            for u in range(2):
                step = STEPS - 1 - (it * 2 + u)
                d_now, x_now, c_now = dm[step], dx[step], ct[step]
                rows = pl.ds(pl.multiple_of(step * 8, 8), 8)
                spot = lane8 == place + step
                if group == 0:
                    sum1 = sum2 = jnp.zeros((8, CH), F32)
                else:
                    sum1, sum2 = get2(g1, rows), get2(g2, rows)
                for i, n in enumerate(names):
                    here = twice(cx[step, n]) * c_now + adj[i]
                    adj[i] = dec[n, step] * here
                    product = here * car[n, step]
                    sum1 = sum1 + twice(bx[step, n]) * here
                    sum2 = sum2 + rates[i] * product
                    grads[i] = grads[i] + d_now * product
                    sums[i] = jnp.where(spot, lanes_sum(here * x_now), sums[i])
                put2(g1, rows, sum1)
                put2(g2, rows, sum2)
            return tuple(adj + grads + sums)

        init = [get2(win2, slice(8 * n, 8 * n + 8)) for n in names]
        init += [jnp.zeros((8, CH), F32)] * GROUP
        init += [jnp.zeros((8, LANE), F32)] * GROUP
        out = lax.fori_loop(0, STEPS // 2, body, tuple(init))
        for i, n in enumerate(names):
            rs[n, 0:1, :] = -jnp.sum(out[GROUP + i], axis=0, keepdims=True)
            in_rows(n, 0, out[2 * GROUP + i])

    def first_sums():
        skip = jnp.sum(mc_ref[...].astype(F32) * x_ref[...].astype(F32), axis=0, keepdims=True)
        for n in range(NST):
            rs[n, 1:2, :] = skip
        by_seq = [channel() for _ in range(1, NSEQ)]
        by_ex = [channel() for _ in range(1, NEX)]
        for k in range(1, NEX):
            start(bcl.at[at_ex(k)], bc1.at[e], by_ex[k - 1], {"expert": at_ex(k)})
        for k in range(1, NSEQ):
            start(rs.at[at_seq(k)], rsr.at[z], by_seq[k - 1], {"seq": at_seq(k)})
        bc1[e] = bcl[e]
        rsr[z] = rs[z]
        return by_seq, by_ex

    def second_sums(slots):
        by_seq, by_ex = slots
        for k in range(1, NEX):
            arrive(bc1.at[at_ex(-k)], by_ex[k - 1], {"expert": at_ex(-k)})
        tile = bc1[0]
        for k in range(1, NEX):
            tile = tile + bc1[k]
        bc2[y] = tile
        by_dp = [channel() for _ in range(1, NDP)]
        for k in range(1, NDP):
            start(bc2.at[y], bc2.at[y], by_dp[k - 1], {"dp": at_dp(k)})
        for k in range(1, NSEQ):
            arrive(rsr.at[at_seq(-k)], by_seq[k - 1], {"seq": at_seq(-k)})
        total = rsr[0]
        for p in range(1, NSEQ):
            total = total + rsr[p]
        skipgrad_ref[...] = total[1:2, :]
        rgg[z] = total[0:1, :]
        by_seq = [channel() for _ in range(1, NSEQ)]
        for k in range(1, NSEQ):
            start(rgg.at[z], rgg.at[z], by_seq[k - 1], {"seq": at_seq(k)})
        return by_seq, by_dp

    def third_sums(slots):
        by_seq, by_dp = slots
        for k in range(1, NDP):
            arrive(bc2.at[at_dp(-k)], by_dp[k - 1], {"dp": at_dp(-k)})
        bc3[e] = ((bc2[0] + bc2[1]) + bc2[2]) + bc2[3]
        by_ex = [channel() for _ in range(1, NEX)]
        for k in range(1, NEX):
            start(bc3.at[e], bc3.at[e], by_ex[k - 1], {"expert": at_ex(k)})
        return by_seq, by_ex

    def last_sums(slots):
        by_seq, by_ex = slots
        for k in range(1, NSEQ):
            arrive(rgg.at[at_seq(-k)], by_seq[k - 1], {"seq": at_seq(-k)})
        for n in range(NST):
            rategrad_ref[n : n + 1, :] = rgg[n]
        for k in range(1, NEX):
            arrive(bc3.at[at_ex(-k)], by_ex[k - 1], {"expert": at_ex(-k)})
        for n in range(NST):
            for h in range(2):
                at, cols = 2 * (n % 2) + h, slice(h * LANE, (h + 1) * LANE)
                bgrad_ref[n : n + 1, cols] = bc3[n // 2, at : at + 1, :]
                cgrad_ref[n : n + 1, cols] = bc3[n // 2, at + 4 : at + 5, :]

    def finish_scan():
        for k in range(CHUNKS):
            rows = slice(k * STEPS, (k + 1) * STEPS)
            ours = pl.ds(k, STEPS, stride=CHUNKS)
            sum1, sum2 = get2(g1, ours), get2(g2, ours)
            into = d_ref[rows, :].astype(F32) * sum1 + skip_ref[...] * mc_ref[rows, :].astype(F32)
            ingrad_ref[rows, :] = into.astype(BF16)
            dgrad_ref[rows, :] = (x_ref[rows, :].astype(F32) * sum1 - sum2).astype(BF16)

    def ring_item(name, seq, where=None):
        if name == "b":
            return g.at[y, seq, :, CA:WIDE]
        if name == "b1":
            return g.at[y, seq, :, CA:CB]
        if name == "b2":
            return g.at[y, seq, :, CB:WIDE]
        if name == "a1":
            return g.at[0:2, seq, :, 0:CA]
        return g.at[2:4, seq, :, 0:CA]

    def gather():
        plus, minus = {"seq": at_seq(1)}, {"seq": at_seq(-1)}
        up, down = {"dp": at_dp(1)}, {"dp": at_dp(-1)}
        ring = {}

        def ring_send(name, step, sign):
            seq = at_seq(-sign * (step - 1))
            ring[name, step, sign] = channel()
            start(ring_item(name, seq), ring_item(name, seq), ring[name, step, sign],
                  plus if sign > 0 else minus)

        def ring_wait(name, step, sign):
            arrive(ring_item(name, at_seq(-sign * step)), ring[name, step, sign],
                   minus if sign > 0 else plus)

        across = {}

        def across_send(dist):
            seq = at_seq(dist)
            across[dist] = [channel() for _ in range(4)]
            part = g.at[y, seq, :, CA:WIDE]
            start(part, part, across[dist][0], up)
            start(part, part, across[dist][1], down)

        def across_pass(dist):
            seq = at_seq(dist)
            slots = across[dist]
            arrive(g.at[at_dp(-1), seq, :, CA:WIDE], slots[0], down)
            half = g.at[at_dp(-1), seq, :, CA:CB]
            start(half, half, slots[2], up)
            arrive(g.at[at_dp(1), seq, :, CA:WIDE], slots[1], up)
            half = g.at[at_dp(1), seq, :, CB:WIDE]
            start(half, half, slots[3], down)

        def across_end(dist):
            seq = at_seq(dist)
            slots = across[dist]
            arrive(g.at[at_dp(2), seq, :, CA:CB], slots[2], down)
            arrive(g.at[at_dp(2), seq, :, CB:WIDE], slots[3], up)

        first = [channel() for _ in range(1, NDP)]
        mine = g.at[y, z, :, 0:CA]
        for k in range(1, NDP):
            start(mine, mine, first[k - 1], {"dp": at_dp(k)})
        ring_send("b", 1, 1)
        ring_send("b", 1, -1)
        across_send(0)
        yield
        for k in range(1, NDP):
            arrive(g.at[at_dp(-k), z, :, 0:CA], first[k - 1], {"dp": at_dp(-k)})
        for name in ("a1", "a2"):
            ring_send(name, 1, 1)
            ring_send(name, 1, -1)
        yield
        half = NSEQ // 2
        pending, passed = [0], []
        for step in range(1, half):
            for name in ("b", "a1", "a2"):
                for sign in (1, -1):
                    ring_wait(name, step, sign)
                    if step < half - 1:
                        ring_send(name, step + 1, sign)
                    elif name == "b":
                        ring_send("b1" if sign > 0 else "b2", half, sign)
                    elif (name == "a1") == (sign > 0):
                        ring_send(name, half, sign)
                if name == "b":
                    across_send(-step)
                    across_send(step)
                elif name == "a1":
                    for dist in pending:
                        across_pass(dist)
                else:
                    for dist in passed:
                        across_end(dist)
                    seq_block(passed)
                    pending, passed = [-step, step], pending
                yield
        ring_wait("b1", half, 1)
        ring_wait("b2", half, -1)
        across_send(half)
        yield
        for dist in pending:
            across_pass(dist)
        for dist in passed:
            across_end(dist)
        seq_block(passed)
        yield
        across_pass(half)
        ring_wait("a1", half, 1)
        ring_wait("a2", half, -1)
        for dist in pending:
            across_end(dist)
        seq_block(pending)
        across_end(half)
        seq_block([half])

    def hidden_block(block):
        cols = slice(block * 256, (block + 1) * 256)
        pre = pre_ref[:, cols].astype(F32)
        sig = jax.nn.sigmoid(pre)
        hidden = (pre * sig).astype(BF16)
        hid_t[:, cols] = hidden
        slope_t[:, cols] = sig * (1.0 + pre * (1.0 - sig))
        tall = jnp.concatenate([hidden.astype(F32), jnp.zeros((256 - HID, 256), F32)], axis=0)
        hid_r[block] = tall.T[:, 0:HID].reshape(NSEQ, 16, HID)

    route_slots = [None] + [channel() for _ in range(1, NSEQ)]
    row64 = lax.broadcasted_iota(jnp.int32, (64, LANE), 0)
    eye64 = lax.broadcasted_iota(jnp.int32, (64, LANE), 1) == row64

    def seq_block(dists):
        if not dists:
            return
        seqs = [at_seq(dist) for dist in dists]
        rows = [g[:, seq, :, 0:D].reshape(64, D) for seq in seqs]
        rows = rows[0] if len(rows) == 1 else jnp.concatenate(rows, axis=0)
        product = lax.dot_general(
            rows, w_ref[...], (((1,), (1,)), ((), ())), preferred_element_type=F32
        )
        for i, (dist, seq) in enumerate(zip(dists, seqs)):
            mine = product[64 * i : 64 * i + 64, :]
            scale = g[:, seq, :, D:WIDE].reshape(64, LANE).astype(F32)
            scale = jnp.concatenate([scale, scale[:, 0 : HID - LANE]], axis=1)
            backs[:, seq] = (scale * mine).reshape(NDP, 16, HID)
            total = jnp.sum(hid_r[:, seq].reshape(64, HID) * mine, axis=1, keepdims=True)
            line = jnp.sum(jnp.where(eye64, total, 0.0), axis=0, keepdims=True)
            if dist == 0:
                rr1[z] = line
            else:
                rp[seq] = line
                start(rp.at[seq], rr1.at[z], route_slots[dist % NSEQ], {"seq": seq})

    def slopes():
        for block in range(NDP):
            cols = slice(block * 256, (block + 1) * 256)
            tall = backs[block].reshape(256, HID)
            wide = jnp.concatenate([tall, jnp.zeros((256, 256 - HID), F32)], axis=1).T
            pregrad_ref[:, cols] = (wide[0:HID, :] * slope_t[:, cols]).astype(BF16)

    def weight_tile(tile, _):
        width = 512
        cols = pl.ds(pl.multiple_of(tile * width, width), width)
        scale = g[:, :, :, D:WIDE].reshape(1024, LANE).astype(F32)
        scale = jnp.concatenate([scale] * (width // LANE), axis=1)
        rows = g[:, :, :, cols].reshape(1024, width).astype(F32)
        scaled = (rows * scale).astype(BF16)
        wgrad_ref[:, cols] = jnp.dot(
            hid_t[...], scaled, preferred_element_type=F32
        ).astype(BF16)
        pltpu.make_async_copy(
            wgrad_ref.at[:, cols], far_out[0].at[:, cols], tsem.at[tile]
        ).start()
        return 0

    def weight_done(tile, _):
        cols = pl.ds(pl.multiple_of(tile * 512, 512), 512)
        pltpu.make_async_copy(
            wgrad_ref.at[:, cols], far_out[0].at[:, cols], tsem.at[tile]
        ).wait()
        return 0

    for i in range(2, 10):
        loads[i].wait()
    prepare()
    spread()
    for k in range(1, NEX):
        arrive(arecv.at[at_ex(-k)], a2a[k - 1], {"expert": at_ex(-k)})
    for q in range(NEX):
        asm[2 * q : 2 * q + 2, :] = arecv[q]
    g[y, z] = asm[...].astype(BF16)

    gathering = gather()
    tick = functools.partial(next, gathering, None)
    tick()
    for group in range(NST // GROUP):
        first_forward(group)
        first_backward(group)
    slots = summarize()
    tick()
    for i in range(2):
        loads[i].wait()
    for block in range(NDP):
        hidden_block(block)
        tick()
    slots = carry_over(slots)
    tick()
    tick()
    tick()
    enter(slots)
    for group in range(NST // GROUP):
        tick()
        second_forward(group)
    for group in range(NST // GROUP):
        tick()
        second_backward(group)
    tick()
    slots = first_sums()
    finish_scan()
    stores[3].start()
    stores[4].start()
    tick()
    tick()
    tick()
    slots = second_sums(slots)
    stores[8].start()
    tick()
    tick()
    tick()
    slots = third_sums(slots)
    for _ in gathering:
        pass

    lax.fori_loop(0, 4, weight_tile, 0)
    last_sums(slots)
    for i in (5, 6, 7):
        stores[i].start()
    for k in range(1, NSEQ):
        arrive(rr1.at[at_seq(-k)], route_slots[k], {"seq": at_seq(-k)})
    total = rr1[0]
    for p in range(1, NSEQ):
        total = total + rr1[p]
    rr2[y] = total
    by_dp = [channel() for _ in range(1, NDP)]
    for k in range(1, NDP):
        start(rr2.at[y], rr2.at[y], by_dp[k - 1], {"dp": at_dp(k)})
    slopes()
    stores[2].start()
    for k in range(1, NDP):
        arrive(rr2.at[at_dp(-k)], by_dp[k - 1], {"dp": at_dp(-k)})
    rr3[e] = ((rr2[0] + rr2[1]) + rr2[2]) + rr2[3]
    by_ex = [channel() for _ in range(1, NEX)]
    for k in range(1, NEX):
        start(rr3.at[e], rr3.at[e], by_ex[k - 1], {"expert": at_ex(k)})
    lax.fori_loop(4, 8, weight_tile, 0)
    for k in range(1, NEX):
        arrive(rr3.at[at_ex(-k)], by_ex[k - 1], {"expert": at_ex(-k)})

    base = y * 16 + e * 2
    picked = jnp.zeros((8, LANE), F32)
    for c in range(2):
        values = jnp.zeros((1, LANE), F32)
        for x in range(NEX):
            here = lane8[0:1, :] == base + c
            value = jnp.sum(jnp.where(here, rr3[x], 0.0), axis=1, keepdims=True)
            values = jnp.where(lane8[0:1, :] == x, value, values)
        picked = picked + slot_of[c] * values
    for k, names in enumerate((named_first, named_second)):
        total = jnp.sum(picked * names, axis=1, keepdims=True)
        line = jnp.sum(jnp.where(lane8 == sub8, total, 0.0), axis=0, keepdims=True)
        route_ref[k : k + 1, :] = line[:, 0:8]

    stores[1].start()
    lax.fori_loop(0, 8, weight_done, 0)
    for copy in stores[1:]:
        copy.wait()
    for copy in sent:
        copy.wait_send()


def hand_over(*arrays):
    count = len(arrays)

    def body(*refs):
        sources, targets, held = refs[:count], refs[count : 2 * count], refs[2 * count : -2]
        into, out = refs[-2:]
        loads = [
            pltpu.make_async_copy(sources[i], held[i], into.at[i]) for i in range(count)
        ]
        stores = [
            pltpu.make_async_copy(held[i], targets[i], out.at[i]) for i in range(count)
        ]
        for load in loads:
            load.start()
        for load, store in zip(loads, stores):
            load.wait()
            store.start()
        for store in stores:
            store.wait()

    hbm = pl.BlockSpec(memory_space=pltpu.HBM)
    return pl.pallas_call(
        body,
        out_shape=[jax.ShapeDtypeStruct(a.shape, a.dtype) for a in arrays],
        in_specs=[hbm] * count,
        out_specs=[hbm] * count,
        scratch_shapes=[pltpu.VMEM(a.shape, a.dtype) for a in arrays]
        + [pltpu.SemaphoreType.DMA((count,)), pltpu.SemaphoreType.DMA((count,))],
    )(*arrays)


def local(
    moe_cotangent, route_ids, route_weights, saved_pre, w_down, inputs, deltas, mamba_cotangent,
    b_proj, c_proj, decay_rates, skip_gain, documents,
):
    vmem = pl.BlockSpec(memory_space=pltpu.VMEM)
    hbm = pl.BlockSpec(memory_space=pltpu.HBM)

    def out(shape, dtype):
        return jax.ShapeDtypeStruct(shape, dtype)

    def f32(*shape):
        return pltpu.VMEM(shape, F32)

    copies = 320
    arrays = (
        saved_pre[0].T, w_down.reshape(HID, D), inputs, deltas, mamba_cotangent,
        b_proj.T, c_proj.T, decay_rates, skip_gain.reshape(1, CH), documents.reshape(1, TOK),
    )
    results = [
        out((HID, D), BF16),
        out((2, 8), F32),
        out((HID, 1024), BF16),
        out((TOK, CH), BF16),
        out((TOK, CH), BF16),
        out((NST, TOK), F32),
        out((NST, TOK), F32),
        out((NST, CH), F32),
        out((1, CH), F32),
    ]
    wgrad, route, pregrad, ingrad, dgrad, bgrad, cgrad, rategrad, skipgrad = pl.pallas_call(
        kernel,
        out_shape=results,
        in_specs=[vmem] * 3 + [hbm] * len(arrays),
        out_specs=[hbm] * len(results),
        scratch_shapes=[pltpu.VMEM(a.shape, a.dtype) for a in (*arrays, *results)] + [
            pltpu.VMEM((NDP, NSEQ, 16, WIDE), BF16),
            f32(NEX, 2, WIDE), f32(NEX, 2, WIDE), f32(16, WIDE),
            pltpu.VMEM((HID, 1024), BF16), f32(NDP, NSEQ, 16, HID), f32(HID, 1024),
            f32(NDP, NSEQ, 16, HID),
            f32(TOK + 8, LANE),
            f32(2, TOK, LANE), f32(2, TOK, LANE), f32(2, TOK, LANE), f32(2, TOK, LANE),
            f32(STEPS, 8, CH), f32(STEPS, 8, CH), f32(STEPS, 8, CH),
            f32(STEPS, NST, 8, LANE), f32(STEPS, NST, 8, LANE),
            f32(NST, STEPS, 8, CH), f32(NST, STEPS, 8, CH),
            f32(2, TOK, LANE), f32(2, TOK, LANE),
            f32(2, TOK // 2, LANE), f32(2, TOK // 2, LANE),
            f32(2, TOK // 2, LANE), f32(2, TOK // 2, LANE),
            f32(NST, 4, CH), f32(NSEQ, 4, CH), f32(NSEQ, 2, CH), f32(NST, 2, CH),
            f32(NST, CH), f32(NST, CH),
            f32(8, 8, LANE), f32(8, 8, LANE), f32(NDP, 8, LANE), f32(8, 8, LANE),
            f32(NST, 2, CH), f32(NSEQ, 2, CH), f32(NST, 1, CH),
            f32(NSEQ, 1, LANE), f32(NSEQ, 1, LANE), f32(NDP, 1, LANE), f32(NEX, 1, LANE),
            pltpu.SemaphoreType.DMA((copies,)),
            pltpu.SemaphoreType.DMA((copies,)),
            pltpu.SemaphoreType.DMA((len(arrays),)),
            pltpu.SemaphoreType.DMA((len(results),)),
            pltpu.SemaphoreType.DMA((8,)),
        ],
        compiler_params=pltpu.CompilerParams(
            collective_id=0, has_side_effects=True, vmem_limit_bytes=56 * 1024 * 1024
        ),
    )(
        moe_cotangent, route_ids.T, route_weights.T, *arrays
    )
    wgrad, route, pregrad, ingrad, dgrad, bgrad, cgrad, rategrad, skipgrad = hand_over(
        wgrad, route, pregrad, ingrad, dgrad, bgrad, cgrad, rategrad, skipgrad
    )
    return (
        wgrad.reshape(1, HID, D),
        route.T,
        pregrad.T.reshape(1, 1024, HID),
        ingrad,
        dgrad,
        bgrad.T,
        cgrad.T,
        rategrad,
        skipgrad.reshape(CH),
    )


def solution(mesh):
    return jax.shard_map(
        local,
        mesh=mesh,
        in_specs=(
            P(("dp", "seq", "expert"), None),
            P(("dp", "seq", "expert"), None),
            P(("dp", "seq", "expert"), None),
            P("expert", None, ("dp", "seq")),
            P("expert", ("dp", "seq"), None),
            P("seq", ("dp", "expert")),
            P("seq", ("dp", "expert")),
            P("seq", ("dp", "expert")),
            P("seq", None),
            P("seq", None),
            P(None, ("dp", "expert")),
            P(("dp", "expert")),
            P("seq"),
        ),
        out_specs=(
            P("expert", ("dp", "seq"), None),
            P(("dp", "seq", "expert"), None),
            P("expert", None, ("dp", "seq")),
            P("seq", ("dp", "expert")),
            P("seq", ("dp", "expert")),
            P("seq", None),
            P("seq", None),
            P(None, ("dp", "expert")),
            P(("dp", "expert")),
        ),
        check_vma=False,
    )
```

```python
import functools

import jax
import jax.numpy as jnp
from jax import lax
from jax.experimental import pallas as pl
from jax.experimental.pallas import tpu as pltpu
from jax.sharding import PartitionSpec as P

F32, BF16 = jnp.float32, jnp.bfloat16
MESH = pl.DeviceIdType.MESH
NDP, NSEQ, NEX = 4, 16, 8
D, HID, NST, CH, TOK = 4096, 192, 16, 256, 256
LANE = 128
WIDE = D + LANE
CA = 10 * LANE
CB = CA + 12 * LANE
CHUNKS, STEPS = 8, TOK // 8
GROUP = 4
BIG = 1e9
ORDER = (
    "b1", "x1", "p0", "b2", "p1", "y1", "d0", "b3", "x2", "p2", "d1", "b4", "y2", "p3", "d2",
    "b5", "x3", "b6", "p4", "y3", "d3", "b7", "x4", "p5", "b8", "y4", "d4", "p6", "x5",
    "y5", "d5", "x6", "p7", "y6", "d6", "x7", "p8", "y7", "d7", "x8", "d8",
)


def get2(ref, rows):
    return jnp.concatenate([ref[0, rows, :], ref[1, rows, :]], axis=1)


def put2(ref, rows, value):
    ref[0, rows, :] = value[:, 0:LANE]
    ref[1, rows, :] = value[:, LANE:CH]


def kernel(
    cot_ref, ids_ref, wts_ref, *refs
):
    count_in, count_out = 10, 9
    far_in, refs = refs[:count_in], refs[count_in:]
    far_out, refs = refs[:count_out], refs[count_out:]
    near_in, refs = refs[:count_in], refs[count_in:]
    near_out, refs = refs[:count_out], refs[count_out:]
    pre_ref, w_ref, x_ref, d_ref, mc_ref, b_ref, c_ref, rate_ref, skip_ref, doc_ref = near_in
    (
        wgrad_ref, route_ref, pregrad_ref, ingrad_ref, dgrad_ref, bgrad_ref, cgrad_ref,
        rategrad_ref, skipgrad_ref,
    ) = near_out
    (
        g, asend, arecv, asm, hid_t, hid_r, slope_t, backs,
        docs, bc2d, dm2, dx2, ct2, dm, dx, ct, bx, cx, perm, dec, car, g1, g2,
        ssum, wsum, sin2, win2, summ, gath, ret, back, sbuf, wbuf,
        bcl, bc1, bc2, bc3, rs, rsr, rgg, rp, rr1, rr3,
        ssem, rsem, isem, osem, tsem,
    ) = refs
    loads = [
        pltpu.make_async_copy(far, near, isem.at[i])
        for i, (far, near) in enumerate(zip(far_in, near_in))
    ]
    stores = [None] + [
        pltpu.make_async_copy(near_out[i], far_out[i], osem.at[i]) for i in range(1, count_out)
    ]

    y, z, e = lax.axis_index("dp"), lax.axis_index("seq"), lax.axis_index("expert")
    counter = [0]
    sent = []

    def at_seq(k):
        return lax.rem(z + k + 2 * NSEQ, NSEQ)

    def at_dp(k):
        return lax.rem(y + k + 2 * NDP, NDP)

    def at_ex(k):
        return lax.rem(e + k + 2 * NEX, NEX)

    def channel():
        counter[0] += 1
        return counter[0] - 1

    def start(src, dst, slot, device):
        copy = pltpu.make_async_remote_copy(
            src_ref=src, dst_ref=dst, send_sem=ssem.at[slot], recv_sem=rsem.at[slot],
            device_id=device, device_id_type=MESH,
        )
        copy.start()
        sent.append(copy)

    def arrive(dst, slot, device):
        pltpu.make_async_remote_copy(
            src_ref=dst, dst_ref=dst, send_sem=ssem.at[slot], recv_sem=rsem.at[slot],
            device_id=device, device_id_type=MESH,
        ).wait_recv()

    barrier = pltpu.get_barrier_semaphore()
    peers = [{"seq": at_seq(k)} for k in range(1, NSEQ)]
    peers += [{"dp": at_dp(k)} for k in range(1, NDP)]
    peers += [{"expert": at_ex(k)} for k in range(1, NEX)]
    peers += [
        {"dp": at_dp(k), "expert": at_ex(j)} for k in range(1, NDP) for j in range(1, NEX)
    ]
    for peer in peers:
        pl.semaphore_signal(barrier, inc=1, device_id=peer, device_id_type=MESH)

    for i in (2, 3, 4, 5, 6, 7, 8, 9, 0, 1):
        loads[i].start()

    lane8 = lax.broadcasted_iota(jnp.int32, (8, LANE), 1)
    sub8 = lax.broadcasted_iota(jnp.int32, (8, LANE), 0)
    eye8 = lane8[:, 0:8] == sub8[:, 0:8]

    def column(row):
        return jnp.sum(
            jnp.where(eye8, jnp.broadcast_to(row, (8, 8)), 0.0), axis=1, keepdims=True
        )

    lanes32 = lane8.astype(F32)
    named_first = (lanes32 == column(ids_ref[0:1, :].astype(F32))).astype(F32)
    named_second = (lanes32 == column(ids_ref[1:2, :].astype(F32))).astype(F32)
    named = jnp.maximum(named_first, named_second)
    before = jnp.zeros((8, LANE), F32)
    for t in range(7):
        before += jnp.where(sub8 > t, named[t : t + 1, :], 0.0)
    slot_of = [
        jnp.where(before == float(c), named, 0.0) for c in range(2)
    ]
    weights = wts_ref[...].astype(F32)
    pair_weight = named_first * column(weights[0:1, :]) + named_second * column(weights[1:2, :])
    rows32 = cot_ref[...].astype(F32)
    for x in range(NEX):
        for c in range(2):
            chosen = slot_of[c][:, x : x + 1]
            asend[x, c : c + 1, 0:D] = jnp.sum(chosen * rows32, axis=0, keepdims=True)
            share = jnp.sum(
                (slot_of[c] * pair_weight)[:, x : x + 1] * jnp.ones((8, LANE), F32),
                axis=0, keepdims=True,
            )
            asend[x, c : c + 1, D:WIDE] = share

    pl.semaphore_wait(barrier, len(peers))

    a2a = [channel() for _ in range(1, NEX)]
    for k in range(1, NEX):
        start(asend.at[at_ex(k)], arecv.at[e], a2a[k - 1], {"expert": at_ex(k)})
    arecv[e] = asend[e]

    def prepare():
        for h in range(2):
            row = doc_ref[:, h * LANE : (h + 1) * LANE].astype(F32)
            docs[8 + h * LANE : 8 + (h + 1) * LANE, :] = jnp.broadcast_to(row, (LANE, LANE)).T
        doc = docs[8 : TOK + 8, :]
        docs[7:8, :] = doc[0:1, :]
        keep = docs[7 : TOK + 7, :] == doc
        for h in range(2):
            cols = slice(h * LANE, (h + 1) * LANE)
            d32 = d_ref[:, cols].astype(F32)
            dm2[h] = jnp.where(keep, d32, BIG)
            dx2[h] = d32 * x_ref[:, cols].astype(F32)
            ct2[h] = mc_ref[:, cols].astype(F32)
            for i, ref in enumerate((b_ref, c_ref)):
                rest, parts = ref[:, cols], []
                for _ in range(3):
                    parts.append(rest.astype(BF16).astype(F32))
                    rest = rest - parts[-1]
                parts.append(jnp.zeros((LANE - 3 * NST, LANE), F32))
                bc2d[i, cols, :] = jnp.concatenate(parts, axis=0).T

    def spread():
        def body(step, _):
            rows = pl.ds(step, CHUNKS, stride=STEPS)
            dm[step] = get2(dm2, rows)
            dx[step] = get2(dx2, rows)
            ct[step] = get2(ct2, rows)
            eight = pl.ds(pl.multiple_of(step * 8, 8), 8)
            perm[0, eight, :] = bc2d[0, rows, :]
            perm[1, eight, :] = bc2d[1, rows, :]
            return 0

        lax.fori_loop(0, STEPS, body, 0)
        part = lax.broadcasted_iota(jnp.int32, (LANE, 4 * LANE), 0)
        lane = lax.broadcasted_iota(jnp.int32, (LANE, 4 * LANE), 1)
        for quarter in range(NST // 4):
            state = quarter * 4 + lane // LANE
            choice = ((part % NST == state) & (part < 3 * NST)).astype(F32).astype(BF16)
            cols = slice(quarter * 4 * LANE, (quarter + 1) * 4 * LANE)
            for ref, i in ((bx, 0), (cx, 1)):
                ref[:, cols] = jnp.dot(
                    perm[i].astype(BF16), choice, preferred_element_type=F32
                )

    def spot_of(step, n):
        return pl.ds(pl.multiple_of(step * 8, 8), 8), slice(n * LANE, (n + 1) * LANE)

    def twice(v):
        return jnp.concatenate([v, v], axis=1)

    def rate_of(n):
        return jnp.broadcast_to(rate_ref[n : n + 1, :], (8, CH)) * -1.4426950408889634

    def first_forward(group):
        names = [group * GROUP + i for i in range(GROUP)]
        scale = [rate_of(n) for n in names]

        def body(it, carry):
            carry = list(carry)
            for u in range(2):
                step = it * 2 + u
                d_now, x_now = dm[step], dx[step]
                for i, n in enumerate(names):
                    decay = jnp.exp2(d_now * scale[i])
                    dec[n, step] = decay
                    carry[i] = decay * carry[i] + twice(bx[spot_of(step, n)]) * x_now
            return tuple(carry)

        out = lax.fori_loop(0, STEPS // 2, body, tuple(jnp.zeros((8, CH), F32) for _ in names))
        for i, n in enumerate(names):
            put2(ssum, slice(8 * n, 8 * n + 8), out[i])

    def first_backward(group):
        names = [group * GROUP + i for i in range(GROUP)]

        def body(it, carry):
            carry = list(carry)
            for u in range(2):
                step = STEPS - 1 - (it * 2 + u)
                c_now = ct[step]
                for i, n in enumerate(names):
                    carry[i] = dec[n, step] * (twice(cx[spot_of(step, n)]) * c_now + carry[i])
            return tuple(carry)

        out = lax.fori_loop(0, STEPS // 2, body, tuple(jnp.zeros((8, CH), F32) for _ in names))
        for i, n in enumerate(names):
            put2(wsum, slice(8 * n, 8 * n + 8), out[i])

    through = []

    def chunk_rows(k):
        return pl.ds(k, NST, stride=CHUNKS)

    def summarize():
        total = jnp.zeros((8, CH), F32)
        total = lax.fori_loop(0, STEPS, lambda s, acc: acc + dm[s], total)
        scale = rate_ref[...] * -1.4426950408889634
        for k in range(CHUNKS):
            through.append(jnp.exp2(scale * total[k : k + 1, :]))
        state = jnp.zeros((NST, CH), F32)
        whole = jnp.ones((NST, CH), F32)
        for k in range(CHUNKS):
            state = get2(ssum, chunk_rows(k)) + through[k] * state
            whole = whole * through[k]
        adjoint = jnp.zeros((NST, CH), F32)
        for k in reversed(range(CHUNKS)):
            adjoint = get2(wsum, chunk_rows(k)) + through[k] * adjoint
        ends = jnp.concatenate([docs[8:9, :], docs[TOK + 7 : TOK + 8, :]], axis=1)
        for n in range(NST):
            summ[n, 0:1, :] = whole[n : n + 1, :]
            summ[n, 1:2, :] = state[n : n + 1, :]
            summ[n, 2:3, :] = adjoint[n : n + 1, :]
            summ[n, 3:4, :] = ends
        slots = [channel() for _ in range(1, NSEQ)]
        for k in range(1, NSEQ):
            start(summ.at[at_seq(k)], gath.at[z], slots[k - 1], {"seq": at_seq(k)})
        gath[z] = summ[z]
        return slots

    def carry_over(slots):
        for k in range(1, NSEQ):
            arrive(gath.at[at_seq(-k)], slots[k - 1], {"seq": at_seq(-k)})
        same = [jnp.zeros((1, CH), F32)]
        for p in range(1, NSEQ):
            here = gath[p, 3:4, 0:LANE]
            there = gath[p - 1, 3:4, LANE:CH]
            same.append(twice((here == there).astype(F32)))
        same.append(jnp.zeros((1, CH), F32))
        state = jnp.zeros((1, CH), F32)
        for p in range(NSEQ):
            entering = same[p] * state
            ret[p, 0:1, :] = entering
            state = gath[p, 1:2, :] + gath[p, 0:1, :] * entering
        adjoint = jnp.zeros((1, CH), F32)
        for p in reversed(range(NSEQ)):
            entering = same[p + 1] * adjoint
            ret[p, 1:2, :] = entering
            adjoint = gath[p, 2:3, :] + gath[p, 0:1, :] * entering
        slots = [channel() for _ in range(1, NSEQ)]
        for k in range(1, NSEQ):
            start(ret.at[at_seq(k)], back.at[z], slots[k - 1], {"seq": at_seq(k)})
        back[z] = ret[z]
        return slots

    def enter(slots):
        for k in range(1, NSEQ):
            arrive(back.at[at_seq(-k)], slots[k - 1], {"seq": at_seq(-k)})
        for n in range(NST):
            sbuf[n : n + 1, :] = back[n, 0:1, :]
            wbuf[n : n + 1, :] = back[n, 1:2, :]
        state = sbuf[...]
        for k in range(CHUNKS):
            put2(sin2, chunk_rows(k), state)
            state = get2(ssum, chunk_rows(k)) + through[k] * state
        adjoint = wbuf[...]
        for k in reversed(range(CHUNKS)):
            put2(win2, chunk_rows(k), adjoint)
            adjoint = get2(wsum, chunk_rows(k)) + through[k] * adjoint

    place = (sub8 % 4) * STEPS

    def in_rows(n, first, value):
        at = first + 2 * (n % 2)
        bcl[n // 2, at : at + 1, :] = jnp.sum(value[0:4, :], axis=0, keepdims=True)
        bcl[n // 2, at + 1 : at + 2, :] = jnp.sum(value[4:8, :], axis=0, keepdims=True)

    def lanes_sum(v):
        return jnp.sum(v[:, 0:LANE] + v[:, LANE:CH], axis=1, keepdims=True)

    def second_forward(group):
        names = [group * GROUP + i for i in range(GROUP)]

        def body(it, carry):
            states, sums = list(carry[:GROUP]), list(carry[GROUP:])
            for u in range(2):
                step = it * 2 + u
                x_now, c_now = dx[step], ct[step]
                here = lane8 == place + step
                for i, n in enumerate(names):
                    carried = dec[n, step] * states[i]
                    car[n, step] = carried
                    states[i] = carried + twice(bx[spot_of(step, n)]) * x_now
                    total = lanes_sum(states[i] * c_now)
                    sums[i] = jnp.where(here, total, sums[i])
            return tuple(states + sums)

        init = [get2(sin2, slice(8 * n, 8 * n + 8)) for n in names]
        init += [jnp.zeros((8, LANE), F32)] * GROUP
        out = lax.fori_loop(0, STEPS // 2, body, tuple(init))
        for i, n in enumerate(names):
            in_rows(n, 4, out[GROUP + i])

    def second_backward(group):
        names = [group * GROUP + i for i in range(GROUP)]
        rates = [jnp.broadcast_to(rate_ref[n : n + 1, :], (8, CH)) for n in names]

        def body(it, carry):
            adj = list(carry[:GROUP])
            grads = list(carry[GROUP : 2 * GROUP])
            sums = list(carry[2 * GROUP :])
            for u in range(2):
                step = STEPS - 1 - (it * 2 + u)
                d_now, x_now, c_now = dm[step], dx[step], ct[step]
                rows = pl.ds(pl.multiple_of(step * 8, 8), 8)
                spot = lane8 == place + step
                if group == 0:
                    sum1 = sum2 = jnp.zeros((8, CH), F32)
                else:
                    sum1, sum2 = get2(g1, rows), get2(g2, rows)
                for i, n in enumerate(names):
                    here = twice(cx[spot_of(step, n)]) * c_now + adj[i]
                    adj[i] = dec[n, step] * here
                    product = here * car[n, step]
                    sum1 = sum1 + twice(bx[spot_of(step, n)]) * here
                    sum2 = sum2 + rates[i] * product
                    grads[i] = grads[i] + d_now * product
                    sums[i] = jnp.where(spot, lanes_sum(here * x_now), sums[i])
                put2(g1, rows, sum1)
                put2(g2, rows, sum2)
            return tuple(adj + grads + sums)

        init = [get2(win2, slice(8 * n, 8 * n + 8)) for n in names]
        init += [jnp.zeros((8, CH), F32)] * GROUP
        init += [jnp.zeros((8, LANE), F32)] * GROUP
        out = lax.fori_loop(0, STEPS // 2, body, tuple(init))
        for i, n in enumerate(names):
            rs[n, 0:1, :] = -jnp.sum(out[GROUP + i], axis=0, keepdims=True)
            in_rows(n, 0, out[2 * GROUP + i])

    def first_sums():
        skip = jnp.sum(mc_ref[...].astype(F32) * x_ref[...].astype(F32), axis=0, keepdims=True)
        for n in range(NST):
            rs[n, 1:2, :] = skip
        by_seq = [channel() for _ in range(1, NSEQ)]
        by_ex = [channel() for _ in range(1, NEX)]
        for k in range(1, NEX):
            start(bcl.at[at_ex(k)], bc1.at[e], by_ex[k - 1], {"expert": at_ex(k)})
        for k in range(1, NSEQ):
            start(rs.at[at_seq(k)], rsr.at[z], by_seq[k - 1], {"seq": at_seq(k)})
        bc1[e] = bcl[e]
        rsr[z] = rs[z]
        return by_seq, by_ex

    def second_sums(slots):
        by_seq, by_ex = slots
        for k in range(1, NEX):
            arrive(bc1.at[at_ex(-k)], by_ex[k - 1], {"expert": at_ex(-k)})
        tile = bc1[0]
        for k in range(1, NEX):
            tile = tile + bc1[k]
        bc2[y] = tile
        by_dp = [channel() for _ in range(1, NDP)]
        for k in range(1, NDP):
            start(bc2.at[y], bc2.at[y], by_dp[k - 1], {"dp": at_dp(k)})
        for k in range(1, NSEQ):
            arrive(rsr.at[at_seq(-k)], by_seq[k - 1], {"seq": at_seq(-k)})
        total = rsr[0]
        for p in range(1, NSEQ):
            total = total + rsr[p]
        skipgrad_ref[...] = total[1:2, :]
        rgg[z] = total[0:1, :]
        by_seq = [channel() for _ in range(1, NSEQ)]
        for k in range(1, NSEQ):
            start(rgg.at[z], rgg.at[z], by_seq[k - 1], {"seq": at_seq(k)})
        return by_seq, by_dp

    def third_sums(slots):
        by_seq, by_dp = slots
        for k in range(1, NDP):
            arrive(bc2.at[at_dp(-k)], by_dp[k - 1], {"dp": at_dp(-k)})
        bc3[e] = ((bc2[0] + bc2[1]) + bc2[2]) + bc2[3]
        by_ex = [channel() for _ in range(1, NEX)]
        for k in range(1, NEX):
            start(bc3.at[e], bc3.at[e], by_ex[k - 1], {"expert": at_ex(k)})
        return by_seq, by_ex

    def last_sums(slots):
        by_seq, by_ex = slots
        for k in range(1, NSEQ):
            arrive(rgg.at[at_seq(-k)], by_seq[k - 1], {"seq": at_seq(-k)})
        for n in range(NST):
            rategrad_ref[n : n + 1, :] = rgg[n]
        for k in range(1, NEX):
            arrive(bc3.at[at_ex(-k)], by_ex[k - 1], {"expert": at_ex(-k)})
        for n in range(NST):
            for h in range(2):
                at, cols = 2 * (n % 2) + h, slice(h * LANE, (h + 1) * LANE)
                bgrad_ref[n : n + 1, cols] = bc3[n // 2, at : at + 1, :]
                cgrad_ref[n : n + 1, cols] = bc3[n // 2, at + 4 : at + 5, :]

    def finish_scan():
        for k in range(CHUNKS):
            rows = slice(k * STEPS, (k + 1) * STEPS)
            ours = pl.ds(k, STEPS, stride=CHUNKS)
            sum1, sum2 = get2(g1, ours), get2(g2, ours)
            into = d_ref[rows, :].astype(F32) * sum1 + skip_ref[...] * mc_ref[rows, :].astype(F32)
            ingrad_ref[rows, :] = into.astype(BF16)
            dgrad_ref[rows, :] = (x_ref[rows, :].astype(F32) * sum1 - sum2).astype(BF16)

    def ring_item(name, seq, where=None):
        if name == "b":
            return g.at[y, seq, :, CA:WIDE]
        if name == "b1":
            return g.at[y, seq, :, CA:CB]
        if name == "b2":
            return g.at[y, seq, :, CB:WIDE]
        return g.at[at_dp(int(name)), seq, :, 0:CA]

    def gather():
        plus, minus = {"seq": at_seq(1)}, {"seq": at_seq(-1)}
        up, down = {"dp": at_dp(1)}, {"dp": at_dp(-1)}
        ring = {}

        def ring_send(name, step, sign):
            seq = at_seq(-sign * (step - 1))
            ring[name, step, sign] = channel()
            start(ring_item(name, seq), ring_item(name, seq), ring[name, step, sign],
                  plus if sign > 0 else minus)

        def ring_wait(name, step, sign):
            arrive(ring_item(name, at_seq(-sign * step)), ring[name, step, sign],
                   minus if sign > 0 else plus)

        crossing = {}

        def across_send(dist):
            seq = at_seq(dist)
            crossing[dist] = [channel() for _ in range(4)]
            part = g.at[y, seq, :, CA:WIDE]
            start(part, part, crossing[dist][0], up)
            start(part, part, crossing[dist][1], down)

        def across_pass(dist):
            seq = at_seq(dist)
            slots = crossing[dist]
            arrive(g.at[at_dp(-1), seq, :, CA:WIDE], slots[0], down)
            half = g.at[at_dp(-1), seq, :, CA:CB]
            start(half, half, slots[2], up)
            arrive(g.at[at_dp(1), seq, :, CA:WIDE], slots[1], up)
            half = g.at[at_dp(1), seq, :, CB:WIDE]
            start(half, half, slots[3], down)

        def across_end(dist):
            seq = at_seq(dist)
            slots = crossing[dist]
            arrive(g.at[at_dp(2), seq, :, CA:CB], slots[2], down)
            arrive(g.at[at_dp(2), seq, :, CB:WIDE], slots[3], up)

        first = [channel() for _ in range(1, NDP)]
        mine = g.at[y, z, :, 0:CA]
        for k in range(1, NDP):
            start(mine, mine, first[k - 1], {"dp": at_dp(k)})
        ring_send("b", 1, 1)
        ring_send("b", 1, -1)
        across_send(0)
        ring_send("0", 1, 1)
        ring_send("0", 1, -1)
        yield
        for k in range(1, NDP):
            arrive(g.at[at_dp(-k), z, :, 0:CA], first[k - 1], {"dp": at_dp(-k)})
        for name in "123":
            ring_send(name, 1, 1)
            ring_send(name, 1, -1)
        yield
        half = NSEQ // 2

        def both(step):
            return {0: [0], half: [half]}.get(step, [-step, step])

        def ring_b(step):
            if step == half:
                ring_wait("b1", half, 1)
                ring_wait("b2", half, -1)
            else:
                for sign in (1, -1):
                    ring_wait("b", step, sign)
                    if step < half - 1:
                        ring_send("b", step + 1, sign)
                    else:
                        ring_send("b1" if sign > 0 else "b2", half, sign)
            for dist in both(step):
                across_send(dist)

        def ring_a(name, step):
            for sign in (1, -1):
                near = (name in "01") == (sign > 0)
                if step < half or near:
                    ring_wait(name, step, sign)
                if step < half - 1 or (step == half - 1 and near):
                    ring_send(name, step + 1, sign)

        def across(step):
            for dist in both(step):
                across_pass(dist)

        def done(step):
            for dist in both(step):
                across_end(dist)
            seq_block(both(step))

        for turn in ORDER:
            kind, step = turn[:-1], int(turn[-1])
            if kind == "b":
                ring_b(step)
                yield
            elif kind == "p":
                across(step)
            elif kind == "d":
                done(step)
            else:
                for name in {"x": "01", "y": "23"}[kind]:
                    ring_a(name, step)
                if step == half:
                    for name in "23":
                        ring_a(name, step)
                yield

    def hidden_block(block):
        cols = slice(block * 256, (block + 1) * 256)
        pre = pre_ref[:, cols].astype(F32)
        sig = jax.nn.sigmoid(pre)
        hidden = (pre * sig).astype(BF16)
        hid_t[:, cols] = hidden
        slope_t[:, cols] = sig * (1.0 + pre * (1.0 - sig))
        tall = jnp.concatenate([hidden.astype(F32), jnp.zeros((256 - HID, 256), F32)], axis=0)
        hid_r[block] = tall.T[:, 0:HID].reshape(NSEQ, 16, HID)

    route_slots = [None] + [channel() for _ in range(1, NSEQ)]
    row64 = lax.broadcasted_iota(jnp.int32, (64, LANE), 0)
    eye64 = lax.broadcasted_iota(jnp.int32, (64, LANE), 1) == row64

    def seq_block(dists):
        if not dists:
            return
        seqs = [at_seq(dist) for dist in dists]
        rows = [g[:, seq, :, 0:D].reshape(64, D) for seq in seqs]
        rows = rows[0] if len(rows) == 1 else jnp.concatenate(rows, axis=0)
        product = lax.dot_general(
            rows, w_ref[...], (((1,), (1,)), ((), ())), preferred_element_type=F32
        )
        for i, (dist, seq) in enumerate(zip(dists, seqs)):
            mine = product[64 * i : 64 * i + 64, :]
            scale = g[:, seq, :, D:WIDE].reshape(64, LANE).astype(F32)
            scale = jnp.concatenate([scale, scale[:, 0 : HID - LANE]], axis=1)
            backs[:, seq] = (scale * mine).reshape(NDP, 16, HID)
            total = jnp.sum(hid_r[:, seq].reshape(64, HID) * mine, axis=1, keepdims=True)
            line = jnp.sum(jnp.where(eye64, total, 0.0), axis=0, keepdims=True)
            if dist == 0:
                rr1[z] = line
            else:
                rp[seq] = line
                start(rp.at[seq], rr1.at[z], route_slots[dist % NSEQ], {"seq": seq})

    def slopes():
        for block in range(NDP):
            cols = slice(block * 256, (block + 1) * 256)
            tall = backs[block].reshape(256, HID)
            wide = jnp.concatenate([tall, jnp.zeros((256, 256 - HID), F32)], axis=1).T
            pregrad_ref[:, cols] = (wide[0:HID, :] * slope_t[:, cols]).astype(BF16)

    def weight_tile(tile, _):
        width = 512
        cols = pl.ds(pl.multiple_of(tile * width, width), width)
        scale = g[:, :, :, D:WIDE].reshape(1024, LANE)
        scale = jnp.concatenate([scale] * (width // LANE), axis=1)
        scaled = g[:, :, :, cols].reshape(1024, width) * scale
        wgrad_ref[:, cols] = jnp.dot(
            hid_t[...], scaled, preferred_element_type=F32
        ).astype(BF16)
        pltpu.make_async_copy(
            wgrad_ref.at[:, cols], far_out[0].at[:, cols], tsem.at[tile]
        ).start()
        return 0

    def weight_done(tile, _):
        cols = pl.ds(pl.multiple_of(tile * 512, 512), 512)
        pltpu.make_async_copy(
            wgrad_ref.at[:, cols], far_out[0].at[:, cols], tsem.at[tile]
        ).wait()
        return 0

    for i in range(2, 10):
        loads[i].wait()
    prepare()
    spread()
    for k in range(1, NEX):
        arrive(arecv.at[at_ex(-k)], a2a[k - 1], {"expert": at_ex(-k)})
    for q in range(NEX):
        asm[2 * q : 2 * q + 2, :] = arecv[q]
    g[y, z] = asm[...].astype(BF16)

    gathering = gather()
    tick = functools.partial(next, gathering, None)
    tick()
    for group in range(NST // GROUP):
        first_forward(group)
        first_backward(group)
    slots = summarize()
    tick()
    for i in range(2):
        loads[i].wait()
    for block in range(NDP):
        hidden_block(block)
        tick()
    slots = carry_over(slots)
    tick()
    tick()
    tick()
    enter(slots)
    for group in range(NST // GROUP):
        tick()
        second_forward(group)
    for group in range(NST // GROUP):
        tick()
        second_backward(group)
    tick()
    slots = first_sums()
    finish_scan()
    stores[3].start()
    stores[4].start()
    tick()
    tick()
    tick()
    slots = second_sums(slots)
    stores[8].start()
    tick()
    tick()
    tick()
    slots = third_sums(slots)
    for _ in gathering:
        pass

    lax.fori_loop(0, 4, weight_tile, 0)
    last_sums(slots)
    for i in (5, 6, 7):
        stores[i].start()
    for k in range(1, NSEQ):
        arrive(rr1.at[at_seq(-k)], route_slots[k], {"seq": at_seq(-k)})
    total = rr1[0]
    for p in range(1, NSEQ):
        total = total + rr1[p]
    rr3[y * NEX + e] = total
    others = [(k, j) for k in range(NDP) for j in range(NEX) if (k, j) != (0, 0)]
    last = {pair: channel() for pair in others}
    for k, j in others:
        start(rr3.at[y * NEX + e], rr3.at[y * NEX + e], last[k, j],
              {"dp": at_dp(k), "expert": at_ex(j)})
    slopes()
    stores[2].start()
    lax.fori_loop(4, 8, weight_tile, 0)
    for k, j in others:
        arrive(rr3.at[at_dp(-k) * NEX + at_ex(-j)], last[k, j],
               {"dp": at_dp(-k), "expert": at_ex(-j)})
    tables = [
        ((rr3[x] + rr3[NEX + x]) + rr3[2 * NEX + x]) + rr3[3 * NEX + x] for x in range(NEX)
    ]

    base = y * 16 + e * 2
    picked = jnp.zeros((8, LANE), F32)
    for c in range(2):
        values = jnp.zeros((1, LANE), F32)
        for x in range(NEX):
            here = lane8[0:1, :] == base + c
            value = jnp.sum(jnp.where(here, tables[x], 0.0), axis=1, keepdims=True)
            values = jnp.where(lane8[0:1, :] == x, value, values)
        picked = picked + slot_of[c] * values
    for k, names in enumerate((named_first, named_second)):
        total = jnp.sum(picked * names, axis=1, keepdims=True)
        line = jnp.sum(jnp.where(lane8 == sub8, total, 0.0), axis=0, keepdims=True)
        route_ref[k : k + 1, :] = line[:, 0:8]

    stores[1].start()
    lax.fori_loop(0, 8, weight_done, 0)
    for copy in stores[1:]:
        copy.wait()
    for copy in sent:
        copy.wait_send()


def hand_over(*arrays):
    count = len(arrays)

    def body(*refs):
        sources, targets, held = refs[:count], refs[count : 2 * count], refs[2 * count : -2]
        into, out = refs[-2:]
        loads = [
            pltpu.make_async_copy(sources[i], held[i], into.at[i]) for i in range(count)
        ]
        stores = [
            pltpu.make_async_copy(held[i], targets[i], out.at[i]) for i in range(count)
        ]
        for load in loads:
            load.start()
        for load, store in zip(loads, stores):
            load.wait()
            store.start()
        for store in stores:
            store.wait()

    hbm = pl.BlockSpec(memory_space=pltpu.HBM)
    return pl.pallas_call(
        body,
        out_shape=[jax.ShapeDtypeStruct(a.shape, a.dtype) for a in arrays],
        in_specs=[hbm] * count,
        out_specs=[hbm] * count,
        scratch_shapes=[pltpu.VMEM(a.shape, a.dtype) for a in arrays]
        + [pltpu.SemaphoreType.DMA((count,)), pltpu.SemaphoreType.DMA((count,))],
    )(*arrays)


def local(
    moe_cotangent, route_ids, route_weights, saved_pre, w_down, inputs, deltas, mamba_cotangent,
    b_proj, c_proj, decay_rates, skip_gain, documents,
):
    vmem = pl.BlockSpec(memory_space=pltpu.VMEM)
    hbm = pl.BlockSpec(memory_space=pltpu.HBM)

    def out(shape, dtype):
        return jax.ShapeDtypeStruct(shape, dtype)

    def f32(*shape):
        return pltpu.VMEM(shape, F32)

    copies = 320
    arrays = (
        saved_pre[0].T, w_down.reshape(HID, D), inputs, deltas, mamba_cotangent,
        b_proj.T, c_proj.T, decay_rates, skip_gain.reshape(1, CH), documents.reshape(1, TOK),
    )
    results = [
        out((HID, D), BF16),
        out((2, 8), F32),
        out((HID, 1024), BF16),
        out((TOK, CH), BF16),
        out((TOK, CH), BF16),
        out((NST, TOK), F32),
        out((NST, TOK), F32),
        out((NST, CH), F32),
        out((1, CH), F32),
    ]
    wgrad, route, pregrad, ingrad, dgrad, bgrad, cgrad, rategrad, skipgrad = pl.pallas_call(
        kernel,
        out_shape=results,
        in_specs=[vmem] * 3 + [hbm] * len(arrays),
        out_specs=[hbm] * len(results),
        scratch_shapes=[pltpu.VMEM(a.shape, a.dtype) for a in (*arrays, *results)] + [
            pltpu.VMEM((NDP, NSEQ, 16, WIDE), BF16),
            f32(NEX, 2, WIDE), f32(NEX, 2, WIDE), f32(16, WIDE),
            pltpu.VMEM((HID, 1024), BF16), f32(NDP, NSEQ, 16, HID), f32(HID, 1024),
            f32(NDP, NSEQ, 16, HID),
            f32(TOK + 8, LANE),
            f32(2, TOK, LANE), f32(2, TOK, LANE), f32(2, TOK, LANE), f32(2, TOK, LANE),
            f32(STEPS, 8, CH), f32(STEPS, 8, CH), f32(STEPS, 8, CH),
            f32(TOK, NST * LANE), f32(TOK, NST * LANE), f32(2, TOK, LANE),
            f32(NST, STEPS, 8, CH), f32(NST, STEPS, 8, CH),
            f32(2, TOK, LANE), f32(2, TOK, LANE),
            f32(2, TOK // 2, LANE), f32(2, TOK // 2, LANE),
            f32(2, TOK // 2, LANE), f32(2, TOK // 2, LANE),
            f32(NST, 4, CH), f32(NSEQ, 4, CH), f32(NSEQ, 2, CH), f32(NST, 2, CH),
            f32(NST, CH), f32(NST, CH),
            f32(8, 8, LANE), f32(8, 8, LANE), f32(NDP, 8, LANE), f32(8, 8, LANE),
            f32(NST, 2, CH), f32(NSEQ, 2, CH), f32(NST, 1, CH),
            f32(NSEQ, 1, LANE), f32(NSEQ, 1, LANE), f32(NDP * NEX, 1, LANE),
            pltpu.SemaphoreType.DMA((copies,)),
            pltpu.SemaphoreType.DMA((copies,)),
            pltpu.SemaphoreType.DMA((len(arrays),)),
            pltpu.SemaphoreType.DMA((len(results),)),
            pltpu.SemaphoreType.DMA((8,)),
        ],
        compiler_params=pltpu.CompilerParams(
            collective_id=0, has_side_effects=True, vmem_limit_bytes=56 * 1024 * 1024
        ),
    )(
        moe_cotangent, route_ids.T, route_weights.T, *arrays
    )
    wgrad, route, pregrad, ingrad, dgrad, bgrad, cgrad, rategrad, skipgrad = hand_over(
        wgrad, route, pregrad, ingrad, dgrad, bgrad, cgrad, rategrad, skipgrad
    )
    return (
        wgrad.reshape(1, HID, D),
        route.T,
        pregrad.T.reshape(1, 1024, HID),
        ingrad,
        dgrad,
        bgrad.T,
        cgrad.T,
        rategrad,
        skipgrad.reshape(CH),
    )


def solution(mesh):
    return jax.shard_map(
        local,
        mesh=mesh,
        in_specs=(
            P(("dp", "seq", "expert"), None),
            P(("dp", "seq", "expert"), None),
            P(("dp", "seq", "expert"), None),
            P("expert", None, ("dp", "seq")),
            P("expert", ("dp", "seq"), None),
            P("seq", ("dp", "expert")),
            P("seq", ("dp", "expert")),
            P("seq", ("dp", "expert")),
            P("seq", None),
            P("seq", None),
            P(None, ("dp", "expert")),
            P(("dp", "expert")),
            P("seq"),
        ),
        out_specs=(
            P("expert", ("dp", "seq"), None),
            P(("dp", "seq", "expert"), None),
            P("expert", None, ("dp", "seq")),
            P("seq", ("dp", "expert")),
            P("seq", ("dp", "expert")),
            P("seq", None),
            P("seq", None),
            P(None, ("dp", "expert")),
            P(("dp", "expert")),
        ),
        check_vma=False,
    )
```
